512 devices in a mesh: tm: 16 (over z_lo, core), space: 32 (over z_hi, x, y).
Axes of the slice: x: 4, y: 4, z: 16 (z_hi: 2, z_lo: 8; z = z_hi * 8 + z_lo), core: 2. Of those that a mesh axis runs over, the one named last changes fastest.
Arguments:
- starts: float32 [16, 512, 16, 512], P('tm', 'space'), may hold values from -6 to 6
- zone_map: int32 [512, 16, 512], P('space'), may hold values from 0 to 15
- zone_velocity: int32 [16], replicated, may hold values from 0 to 15, each once
- conductivity: float32 [16], replicated, may hold values from 0.002 to 0.015
- x_velocity: float32 [16], replicated, may hold values from -0.7 to 0.7
- cross_velocity: float32 [2, 16], replicated, may hold values from -0.1 to 0.1
- coarse_kernel: float32 [3, 3, 3], replicated, may hold values from 0 to 0.2
Outputs:
- corrected: float32 [16, 512, 16, 512], P('tm', 'space')
The draws below stay inside these ranges and needn't reach their ends.
Inputs may be any that keep to these rules, and one draw needn't show every extreme that they name: `zone_velocity`: each of the 16 velocity sets is named by exactly one zone.
All inputs are finite; a program needn't handle non-finite values.
Results may differ from the reference program's by a relative error of at most 0.00002.
Values sent between devices are 32-bit elements; how exact they have to be, the bound alone decides.
A program may use at most 64 MiB of HBM per device.

```python
import math
import jax
import jax.numpy as jnp
from jax import lax

NY = 512
NZ = 16
FINE = 16
ZONES = 16
VELS = 16
SLICES = 16
NX = 512


def draw_starts(key, part):
    key = jax.random.fold_in(key, 5)
    shape = (SLICES, NX, NZ, NY)
    return jnp.clip(jax.random.normal(key, shape, jnp.float32), -6.0, 6.0)


def draw_coarse_kernel(key, part):
    key = jax.random.fold_in(key, 11)
    first_key, second_key = jax.random.split(key)
    raw = jax.random.uniform(first_key, (3, 3, 3), jnp.float32, 0.5, 1.0)
    x_weights = jnp.array([1.0, 0.02, 0.02], jnp.float32)
    raw = raw * x_weights[:, None, None]
    target = jax.random.uniform(second_key, (), jnp.float32, 0.9, 0.97)
    return raw * (target / jnp.sum(raw))


def with_ends(values, own_key, smallest, top_value):
    spot = [jax.random.randint(jax.random.fold_in(own_key, axis), (), 0, length) for axis, length in enumerate(values.shape)]
    main_axis = values.shape.index(max(values.shape))
    next_to = spot[:main_axis] + [(spot[main_axis] + 1) % values.shape[main_axis]] + spot[main_axis + 1:]
    return values.at[tuple(spot)].set(smallest).at[tuple(next_to)].set(top_value)


def setup_inputs(seed: int = 0) -> dict:
    arg_keys = jax.random.split(jax.random.key(seed), 8)
    starts = draw_starts(jax.random.fold_in(arg_keys[7], 71), 0)
    zone_map = with_ends(jax.random.randint(arg_keys[1], (NX, NZ, NY), 0, ZONES), jax.random.fold_in(arg_keys[1], 1), 0, ZONES - 1).astype(jnp.int32)
    zone_velocity = jax.random.permutation(arg_keys[2], ZONES).astype(jnp.int32)
    conductivity = jnp.clip(jnp.exp(jax.random.uniform(arg_keys[3], (ZONES,), jnp.float32, math.log(0.002), math.log(0.015))), 0.002, 0.015)
    x_velocity = jnp.clip(jax.random.uniform(arg_keys[4], (VELS,), jnp.float32, -0.7, 0.7), -0.7, 0.7)
    cross_velocity = jnp.clip(jax.random.uniform(arg_keys[5], (2, VELS), jnp.float32, -0.1, 0.1), -0.1, 0.1)
    coarse_kernel = draw_coarse_kernel(jax.random.fold_in(arg_keys[7], 71), 0)
    return dict(starts=starts, zone_map=zone_map, zone_velocity=zone_velocity, conductivity=conductivity, x_velocity=x_velocity, cross_velocity=cross_velocity, coarse_kernel=coarse_kernel)


def coefficients(zone_map, zone_velocity, conductivity, x_velocity, cross_velocity):
    chosen = (zone_velocity[:, None] == jnp.arange(x_velocity.shape[0], dtype=jnp.int32)[None, :]).astype(jnp.float32)
    lookup = jnp.stack([conductivity,
                        jnp.sum(chosen * x_velocity[None, :], axis=1),
                        jnp.sum(chosen * cross_velocity[1][None, :], axis=1),
                        jnp.sum(chosen * cross_velocity[0][None, :], axis=1)])
    coef_stack = jnp.zeros((4,) + zone_map.shape, jnp.float32)
    for zone_index in range(ZONES):
        coef_stack = coef_stack + jnp.where(zone_map[None] == zone_index, lookup[:, zone_index][:, None, None, None], jnp.float32(0.0))
    return coef_stack


def upwind(courant, values, lower, upper):
    return jnp.maximum(courant, 0.0) * (values - lower) + jnp.minimum(courant, 0.0) * (upper - values)


def advance(values, coef_stack):
    padded = jnp.pad(values, 1)
    x_lower = padded[:-2, 1:-1, 1:-1]
    x_upper = padded[2:, 1:-1, 1:-1]
    z_lower = padded[1:-1, :-2, 1:-1]
    z_upper = padded[1:-1, 2:, 1:-1]
    y_lower = padded[1:-1, 1:-1, :-2]
    y_upper = padded[1:-1, 1:-1, 2:]
    transport = upwind(coef_stack[1], values, x_lower, x_upper)
    transport = transport + upwind(coef_stack[2], values, z_lower, z_upper)
    transport = transport + upwind(coef_stack[3], values, y_lower, y_upper)
    laplace = x_lower + x_upper + z_lower + z_upper + y_lower + y_upper - 6.0 * values
    return values - transport + coef_stack[0] * laplace


def coarse(values, kernel):
    padded = jnp.pad(values, 1)
    total = jnp.zeros_like(values)
    for x_offset in range(3):
        for z_offset in range(3):
            for y_offset in range(3):
                total = total + kernel[x_offset, z_offset, y_offset] * padded[x_offset:x_offset + values.shape[0], z_offset:z_offset + values.shape[1], y_offset:y_offset + values.shape[2]]
    return total


def reference(starts, zone_map, zone_velocity, conductivity, x_velocity, cross_velocity, coarse_kernel):
    coef_stack = coefficients(zone_map, zone_velocity, conductivity, x_velocity, cross_velocity)

    def run_fine(initial):
        return lax.fori_loop(0, FINE, lambda turn_index, current: advance(current, coef_stack), initial)

    fine_ends = lax.map(run_fine, starts)
    outputs = [fine_ends[0]]
    for slice_number in range(1, starts.shape[0]):
        jump_term = fine_ends[slice_number] - coarse(starts[slice_number], coarse_kernel)
        outputs.append(coarse(outputs[-1], coarse_kernel) + jump_term)
    return jnp.stack(outputs)
```

```python
import functools

import jax
import jax.numpy as jnp
from jax import lax
from jax.experimental import pallas as pl
from jax.experimental.pallas import tpu as pltpu
from jax.sharding import PartitionSpec as P

FINE = 16
ZONES = 16
ROWS = 16
NZ = 16
NY = 512
TILES = 4
LANES = 128
EXT = ROWS + 2 * FINE
MESH = pl.DeviceIdType.MESH
HIGH = lax.Precision.HIGHEST


def iotas(shape):
    return lax.broadcasted_iota(jnp.int32, shape, 0), lax.broadcasted_iota(jnp.int32, shape, 1)


def shift_down(v):
    return jnp.concatenate([pltpu.roll(v[:, NY - LANES :], 1, 1), v[:, : NY - LANES]], axis=1)


def shift_up(v):
    return jnp.concatenate([v[:, LANES:], pltpu.roll(v[:, :LANES], LANES - 1, 1)], axis=1)


def coarse_row(src, x, ck):
    zi, li = iotas((NZ, LANES))
    sums = [[], [], []]
    for tile in range(TILES):
        part = [None] * 3
        for a in range(3):
            v = src[x + a - 1, :, tile * LANES : (tile + 1) * LANES]
            below = jnp.where(zi == 0, 0.0, pltpu.roll(v, 1, 0))
            above = jnp.where(zi == NZ - 1, 0.0, pltpu.roll(v, NZ - 1, 0))
            for b, w in enumerate((below, v, above)):
                for c in range(3):
                    term = ck[a, b, c] * w
                    part[c] = term if part[c] is None else part[c] + term
        for c in range(3):
            sums[c].append(part[c])
    low = [jnp.where(li == 0, 0.0, pltpu.roll(sums[0][TILES - 1], 1, 1))] + sums[0][:-1]
    high = sums[2][1:] + [jnp.where(li == LANES - 1, 0.0, pltpu.roll(sums[2][0], LANES - 1, 1))]
    return jnp.concatenate([low[j] + sums[1][j] + high[j] for j in range(TILES)], axis=1)


def kernel(
    zv, cond, xv, cv, ck, starts, zmap, out,
    perm, u, zone, w, gs, ja, jb, cin, ca, cb, co,
    halo_send, halo_recv, ja_send, ja_recv, jb_send, jb_recv, c_send, c_recv, a_send, a_recv,
):
    t = lax.axis_index("tm")
    s = lax.axis_index("space")
    slices = lax.axis_size("tm")
    parts = lax.axis_size("space")
    chip = t // 2
    odd = lax.rem(t, 2) == 1
    even = lax.rem(t, 2) == 0
    has_low = s > 0
    has_high = s < parts - 1
    mate = t + 1 - 2 * lax.rem(t, 2)

    def at(tm, space):
        return {"tm": tm, "space": space}

    barrier = pltpu.get_barrier_semaphore()

    def greet(tm, space):
        pl.semaphore_signal(barrier, inc=1, device_id=at(tm, space), device_id_type=MESH)

    @pl.when(has_low)
    def _():
        greet(t, s - 1)

    @pl.when(has_high)
    def _():
        greet(t, s + 1)

    @pl.when(jnp.logical_and(odd, has_low))
    def _():
        greet(t - 1, s - 1)

    @pl.when(jnp.logical_and(odd, has_high))
    def _():
        greet(t - 1, s + 1)

    greet(mate, s)

    @pl.when(jnp.logical_and(odd, t >= 3))
    def _():
        greet(t - 2, s)

    yi, pi = iotas((NY, NY))
    perm[...] = jnp.where(yi == TILES * lax.rem(pi, LANES) + pi // LANES, 1.0, 0.0)
    own = starts[0].reshape(ROWS * NZ, NY)
    u[0, FINE : FINE + ROWS] = jnp.dot(
        own, perm[...], precision=HIGH, preferred_element_type=jnp.float32
    ).reshape(ROWS, NZ, NY)
    zone[FINE : FINE + ROWS] = jnp.dot(
        zmap[...].reshape(ROWS * NZ, NY).astype(jnp.float32),
        perm[...],
        preferred_element_type=jnp.float32,
    ).reshape(ROWS, NZ, NY)

    zero_row = jnp.zeros((NZ, NY), jnp.float32)

    @pl.when(jnp.logical_not(has_low))
    def _():
        for buf in (u.at[0], u.at[1], cin, ca):
            buf[FINE - 1] = zero_row

    @pl.when(jnp.logical_not(has_high))
    def _():
        for buf in (u.at[0], u.at[1], cin, ca):
            buf[FINE + ROWS] = zero_row

    low_count = has_low.astype(jnp.int32)
    high_count = has_high.astype(jnp.int32)
    near = low_count + high_count
    pl.semaphore_wait(
        barrier,
        near
        + jnp.where(even, near, 0)
        + 1
        + jnp.where(jnp.logical_and(odd, t < slices - 1), 1, 0),
    )

    def halo(kind, up):
        buf = u.at[0] if kind == 0 else zone
        n = 2 * kind + up
        return pltpu.make_async_remote_copy(
            src_ref=buf.at[pl.ds(FINE, ROWS)],
            dst_ref=buf.at[pl.ds(0 if up else FINE + ROWS, ROWS)],
            send_sem=halo_send.at[n],
            recv_sem=halo_recv.at[n],
            device_id=at(t, s + 1 if up else s - 1),
            device_id_type=MESH,
        )

    for kind in (1, 0):

        @pl.when(has_high)
        def _():
            halo(kind, 1).start()

        @pl.when(has_low)
        def _():
            halo(kind, 0).start()

    numbers = []
    for q in range(ZONES):
        v = zv[q]
        numbers.append((cond[q], xv[v], cv[1, v], cv[0, v]))
    zi, li = iotas((NZ, LANES))

    def weights(x, carry):
        for tile in range(TILES):
            sl = slice(tile * LANES, (tile + 1) * LANES)
            z = zone[x, :, sl].astype(jnp.int32)
            bits = [(z & (1 << b)) != 0 for b in range(4)]
            found = []
            for n in range(4):
                level = [numbers[q][n] for q in range(ZONES)]
                for b in range(4):
                    level = [
                        jnp.where(bits[b], level[2 * j + 1], level[2 * j])
                        for j in range(len(level) // 2)
                    ]
                found.append(level[0])
            d, cx, cz, cy = found
            xm = d + jnp.maximum(cx, 0.0)
            xp = d - jnp.minimum(cx, 0.0)
            zm = d + jnp.maximum(cz, 0.0)
            zp = d - jnp.minimum(cz, 0.0)
            ym = d + jnp.maximum(cy, 0.0)
            yp = d - jnp.minimum(cy, 0.0)
            w[0, x, :, sl] = 1.0 - (((xm + xp) + (zm + zp)) + (ym + yp))
            w[1, x, :, sl] = xm
            w[2, x, :, sl] = xp
            w[3, x, :, sl] = jnp.where(zi == 0, 0.0, zm)
            w[4, x, :, sl] = jnp.where(zi == NZ - 1, 0.0, zp)
            if tile == 0:
                ym = jnp.where(li == 0, 0.0, ym)
            if tile == TILES - 1:
                yp = jnp.where(li == LANES - 1, 0.0, yp)
            w[5, x, :, sl] = ym
            w[6, x, :, sl] = yp
        return carry

    lax.fori_loop(FINE, FINE + ROWS, weights, 0)

    def start_coarse(x, carry):
        gs[x - FINE] = coarse_row(u.at[0], x, ck)
        return carry

    lax.fori_loop(FINE + 1, FINE + ROWS - 1, start_coarse, 0)

    @pl.when(has_low)
    def _():
        halo(1, 1).wait_recv()
        halo(0, 1).wait_recv()
        lax.fori_loop(0, FINE, weights, 0)

    @pl.when(has_high)
    def _():
        halo(1, 0).wait_recv()
        halo(0, 0).wait_recv()
        lax.fori_loop(FINE + ROWS, EXT, weights, 0)

    @pl.when(has_low)
    def _():
        halo(1, 0).wait_send()
        halo(0, 0).wait_send()

    @pl.when(has_high)
    def _():
        halo(1, 1).wait_send()
        halo(0, 1).wait_send()

    start_coarse(FINE, 0)
    start_coarse(FINE + ROWS - 1, 0)

    first_row = jnp.where(has_low, 0, FINE)
    end_row = jnp.where(has_high, EXT, FINE + ROWS)

    def step(level, src, dst):
        lo = jnp.maximum(level, first_row)
        hi = jnp.minimum(EXT - level, end_row)

        def row(x, carry):
            v = src[x]
            acc = w[0, x] * v
            acc += w[1, x] * src[x - 1]
            acc += w[2, x] * src[x + 1]
            acc += w[3, x] * pltpu.roll(v, 1, 0)
            acc += w[4, x] * pltpu.roll(v, NZ - 1, 0)
            acc += w[5, x] * shift_down(v)
            acc += w[6, x] * shift_up(v)
            dst[x] = acc
            return carry

        lax.fori_loop(lo, hi, row, 0)

    def two_steps(n, carry):
        step(2 * n + 1, u.at[0], u.at[1])
        step(2 * n + 2, u.at[1], u.at[0])
        return carry

    lax.fori_loop(0, FINE // 2, two_steps, 0)

    keep = jnp.where(t == 0, 0.0, 1.0).astype(jnp.float32)
    depth = slices - 1 - 2 * chip

    def j_copy(x, to_low, to_high, on_even):
        buf = ja if on_even else jb
        send, recv = (ja_send, ja_recv) if on_even else (jb_send, jb_recv)
        space = s - 1 if to_low else (s + 1 if to_high else s)
        to = x + ROWS if to_low else (x - ROWS if to_high else x)
        return pltpu.make_async_remote_copy(
            src_ref=buf.at[FINE + x],
            dst_ref=buf.at[FINE + to],
            send_sem=send.at[0 if to_low else (1 if to_high else 2), x],
            recv_sem=recv.at[FINE + to],
            device_id=at(t + 1 if on_even else t, space),
            device_id_type=MESH,
        )

    def each_jump_copy(x, act):
        @pl.when(even)
        def _():
            @pl.when(jnp.logical_and(has_high, x >= ROWS - depth))
            def _():
                act(j_copy(x, False, True, True))

            @pl.when(jnp.logical_and(has_low, x < depth))
            def _():
                act(j_copy(x, True, False, True))

            act(j_copy(x, False, False, True))

        @pl.when(odd)
        def _():
            @pl.when(jnp.logical_and(has_high, x > ROWS - depth))
            def _():
                act(j_copy(x, False, True, False))

            @pl.when(jnp.logical_and(has_low, x < depth - 1))
            def _():
                act(j_copy(x, True, False, False))

    def make_jump(x, carry):
        value = u[0, FINE + x] - keep * gs[x]

        @pl.when(even)
        def _():
            ja[FINE + x] = value

        @pl.when(odd)
        def _():
            jb[FINE + x] = value

        each_jump_copy(x, lambda copy: copy.start())
        return carry

    lax.fori_loop(0, ROWS, make_jump, 0)

    low_end = jnp.where(has_low, -FINE, 0)
    high_end = jnp.where(has_high, ROWS + FINE - 1, ROWS - 1)
    lo_a = jnp.maximum(-depth, low_end)
    hi_a = jnp.minimum(ROWS - 1 + depth, high_end)
    lo_b = jnp.maximum(1 - depth, low_end)
    hi_b = jnp.minimum(ROWS - 2 + depth, high_end)
    lo_i = jnp.maximum(-depth - 1, low_end)
    hi_i = jnp.minimum(ROWS + depth, high_end)
    passes_on = t < slices - 1

    def c_copy(x):
        return pltpu.make_async_remote_copy(
            src_ref=cb.at[FINE + x],
            dst_ref=cin.at[FINE + x],
            send_sem=c_send.at[FINE + x],
            recv_sem=c_recv.at[FINE + x],
            device_id=at(t + 2, s),
            device_id_type=MESH,
        )

    def a_copy(x):
        return pltpu.make_async_remote_copy(
            src_ref=ca.at[FINE + x],
            dst_ref=co.at[x],
            send_sem=a_send.at[x],
            recv_sem=a_recv.at[x],
            device_id=at(mate, s),
            device_id_type=MESH,
        )

    def j_wait(x, on_even):
        buf, recv = (ja, ja_recv) if on_even else (jb, jb_recv)
        pltpu.make_async_remote_copy(
            src_ref=buf.at[FINE + x],
            dst_ref=buf.at[FINE + x],
            send_sem=(ja_send if on_even else jb_send).at[0, 0],
            recv_sem=recv.at[FINE + x],
            device_id=at(t, s),
            device_id_type=MESH,
        ).wait_recv()

    @pl.when(odd)
    def _():
        @pl.when(chip > 0)
        def _():
            def wait_in(x, carry):
                c_copy(x).wait_recv()
                return carry

            lax.fori_loop(lo_i, lo_a + 1, wait_in, 0)

        def relay(x, carry):
            @pl.when(jnp.logical_and(chip > 0, x + 1 <= hi_i))
            def _():
                c_copy(x + 1).wait_recv()

            @pl.when(x <= hi_a)
            def _():
                j_wait(x, True)

                @pl.when(chip == 0)
                def _():
                    ca[FINE + x] = ja[FINE + x]

                @pl.when(chip > 0)
                def _():
                    ca[FINE + x] = coarse_row(cin, FINE + x, ck) + ja[FINE + x]

            @pl.when(jnp.logical_and(x >= 0, x < ROWS))
            def _():
                a_copy(x).start()

            y = x - 1

            @pl.when(jnp.logical_and(y >= lo_b, y <= hi_b))
            def _():
                @pl.when(jnp.logical_or(y < 0, y >= ROWS))
                def _():
                    j_wait(y, False)

                cb[FINE + y] = coarse_row(ca, FINE + y, ck) + jb[FINE + y]

                @pl.when(passes_on)
                def _():
                    c_copy(y).start()

            return carry

        lax.fori_loop(lo_a, hi_b + 2, relay, 0)
        co[...] = cb[FINE : FINE + ROWS]

    @pl.when(even)
    def _():
        def wait_a(x, carry):
            a_copy(x).wait_recv()
            return carry

        lax.fori_loop(0, ROWS, wait_a, 0)

    out[...] = lax.dot_general(
        co[...].reshape(ROWS * NZ, NY),
        perm[...],
        (((1,), (1,)), ((), ())),
        precision=HIGH,
        preferred_element_type=jnp.float32,
    ).reshape(1, ROWS, NZ, NY)

    def drain_jump(x, carry):
        each_jump_copy(x, lambda copy: copy.wait_send())

        @pl.when(odd)
        def _():
            a_copy(x).wait_send()

        return carry

    lax.fori_loop(0, ROWS, drain_jump, 0)

    @pl.when(jnp.logical_and(odd, passes_on))
    def _():
        def drain(x, carry):
            c_copy(x).wait_send()
            return carry

        lax.fori_loop(lo_b, hi_b + 1, drain, 0)


def shards(
    starts, zone_map, zone_velocity, conductivity, x_velocity, cross_velocity, coarse_kernel
):
    smem = pl.BlockSpec(memory_space=pltpu.SMEM)
    vmem = pl.BlockSpec(memory_space=pltpu.VMEM)
    field = lambda rows: pltpu.VMEM((rows, NZ, NY), jnp.float32)
    dma = pltpu.SemaphoreType.DMA
    return pl.pallas_call(
        kernel,
        name="parareal",
        out_shape=jax.ShapeDtypeStruct(starts.shape, jnp.float32),
        in_specs=[smem] * 5 + [vmem] * 2,
        out_specs=vmem,
        scratch_shapes=[
            pltpu.VMEM((NY, NY), jnp.float32),
            pltpu.VMEM((2, EXT, NZ, NY), jnp.float32),
            field(EXT),
            pltpu.VMEM((7, EXT, NZ, NY), jnp.float32),
            field(ROWS),
            field(EXT),
            field(EXT),
            field(EXT),
            field(EXT),
            field(EXT),
            field(ROWS),
            dma((4,)),
            dma((4,)),
            dma((3, ROWS)),
            dma((EXT,)),
            dma((3, ROWS)),
            dma((EXT,)),
            dma((EXT,)),
            dma((EXT,)),
            dma((ROWS,)),
            dma((ROWS,)),
        ],
        compiler_params=pltpu.CompilerParams(
            collective_id=0, has_side_effects=True, vmem_limit_bytes=56 * 2**20
        ),
    )(
        zone_velocity, conductivity, x_velocity, cross_velocity, coarse_kernel, starts, zone_map
    )


def solution(mesh):
    in_specs = (P("tm", "space", None, None), P("space", None, None), P(), P(), P(), P(), P())
    out_specs = P("tm", "space", None, None)
    return jax.shard_map(shards, mesh=mesh, in_specs=in_specs, out_specs=out_specs, check_vma=False)
```

```python
import functools

import jax
import jax.numpy as jnp
from jax import lax
from jax.experimental import pallas as pl
from jax.experimental.pallas import tpu as pltpu
from jax.sharding import PartitionSpec as P

FINE = 16
ZONES = 16
ROWS = 16
NZ = 16
NY = 512
TILES = 4
LANES = 128
EXT = ROWS + 2 * FINE
BLOCK = 8
PAD = 24
WIDE = ROWS + 2 * PAD
MESH = pl.DeviceIdType.MESH
HIGH = lax.Precision.HIGHEST


def iotas(shape):
    return lax.broadcasted_iota(jnp.int32, shape, 0), lax.broadcasted_iota(jnp.int32, shape, 1)


def shift_down(v):
    return jnp.concatenate([pltpu.roll(v[:, NY - LANES :], 1, 1), v[:, : NY - LANES]], axis=1)


def shift_up(v):
    return jnp.concatenate([v[:, LANES:], pltpu.roll(v[:, :LANES], LANES - 1, 1)], axis=1)


def coarse_row(src, x, ck):
    zi, li = iotas((NZ, LANES))
    sums = [[], [], []]
    for tile in range(TILES):
        part = [None] * 3
        for a in range(3):
            v = src[x + a - 1, :, tile * LANES : (tile + 1) * LANES]
            below = jnp.where(zi == 0, 0.0, pltpu.roll(v, 1, 0))
            above = jnp.where(zi == NZ - 1, 0.0, pltpu.roll(v, NZ - 1, 0))
            for b, w in enumerate((below, v, above)):
                for c in range(3):
                    term = ck[a, b, c] * w
                    part[c] = term if part[c] is None else part[c] + term
        for c in range(3):
            sums[c].append(part[c])
    low = [jnp.where(li == 0, 0.0, pltpu.roll(sums[0][TILES - 1], 1, 1))] + sums[0][:-1]
    high = sums[2][1:] + [jnp.where(li == LANES - 1, 0.0, pltpu.roll(sums[2][0], LANES - 1, 1))]
    return jnp.concatenate([low[j] + sums[1][j] + high[j] for j in range(TILES)], axis=1)


def kernel(
    zv, cond, xv, cv, ck, starts, zmap, out,
    perm, u, first, zone, w, gs, ja, jb, cin, ca, cb, co, rbuf,
    u_send, u_recv, z_send, z_recv, zm_send, zm_recv, zf_send, r_send, r_recv, f_send,
    ja_send, ja_recv, jb_send, jb_recv, jm_send, jm_recv, c_send, c_recv, a_send, a_recv,
):
    t = lax.axis_index("tm")
    s = lax.axis_index("space")
    slices = lax.axis_size("tm")
    parts = lax.axis_size("space")
    chips = slices // 2
    chip = t // 2
    core = lax.rem(t, 2)
    odd = core == 1
    even = core == 0
    has_low = s > 0
    has_high = s < parts - 1
    mate = t + 1 - 2 * core
    half = parts // 2
    far_low = s == half
    far_high = s == half - 1
    far = jnp.logical_or(far_low, far_high)
    over = jnp.where(far_low, s - 1, s + 1)
    ascending = s < half
    end_chip = jnp.logical_or(chip == 0, chip == chips - 1)
    seeds = jnp.logical_and(far, end_chip)
    across = 2 * (chips - 1 - chip) + core
    goes_on = jnp.logical_and(
        far, jnp.logical_and(chip != chips // 2 - 1, chip != chips // 2)
    )
    next_t = jnp.where(chip < chips // 2, t + 2, t - 2)
    last_t = jnp.where(chip < chips // 2, t - 2, t + 2)
    low_helper = [s == half - 5, s == half - 13]
    high_helper = [s == half + 4, s == half + 12]
    helps_up = jnp.logical_or(low_helper[0], low_helper[1])
    helps_down = jnp.logical_or(high_helper[0], high_helper[1])
    helps = jnp.logical_or(helps_up, helps_down)

    def at(tm, space):
        return {"tm": tm, "space": space}

    def both(a, b):
        return jnp.logical_and(a, b)

    def remote(src, dst, send, recv, device):
        return pltpu.make_async_remote_copy(
            src_ref=src,
            dst_ref=dst,
            send_sem=send,
            recv_sem=recv,
            device_id=device,
            device_id_type=MESH,
        )

    barrier = pltpu.get_barrier_semaphore()

    def greet(tm, space):
        pl.semaphore_signal(barrier, inc=1, device_id=at(tm, space), device_id_type=MESH)

    @pl.when(far)
    def _():
        greet(t, jnp.where(far_low, half - 5, half + 4))
        greet(t, jnp.where(far_low, half - 13, half + 12))

        @pl.when(end_chip)
        def _():
            greet(across, over)

        @pl.when(jnp.logical_not(end_chip))
        def _():
            greet(last_t, s)

    @pl.when(helps)
    def _():
        greet(t, jnp.where(helps_up, half - 1, half))

    @pl.when(has_low)
    def _():
        greet(t, s - 1)

    @pl.when(has_high)
    def _():
        greet(t, s + 1)

    @pl.when(both(odd, has_low))
    def _():
        greet(t - 1, s - 1)

    @pl.when(both(odd, has_high))
    def _():
        greet(t - 1, s + 1)

    greet(mate, s)

    @pl.when(both(odd, t >= 3))
    def _():
        greet(t - 2, s)

    yi, pi = iotas((NY, NY))
    perm[...] = jnp.where(yi == TILES * lax.rem(pi, LANES) + pi // LANES, 1.0, 0.0)
    own = starts[0].reshape(ROWS * NZ, NY)
    zone[FINE : FINE + ROWS] = jnp.dot(
        zmap[...].reshape(ROWS * NZ, NY).astype(jnp.float32),
        perm[...],
        preferred_element_type=jnp.float32,
    ).reshape(ROWS, NZ, NY)
    initial = jnp.dot(
        own, perm[...], precision=HIGH, preferred_element_type=jnp.float32
    ).reshape(ROWS, NZ, NY)
    u[0, PAD : PAD + ROWS] = initial
    first[...] = initial

    zero_row = jnp.zeros((NZ, NY), jnp.float32)

    def clear(begin, edge):
        cin[edge] = zero_row
        ca[edge] = zero_row

        def row(x, carry):
            u[0, x] = zero_row
            u[1, x] = zero_row
            for n in range(7):
                w[n, x] = zero_row
            return carry

        lax.fori_loop(begin, begin + PAD - 4, row, 0)

    @pl.when(jnp.logical_not(has_low))
    def _():
        clear(4, FINE - 1)

    @pl.when(jnp.logical_not(has_high))
    def _():
        clear(PAD + ROWS, FINE + ROWS)

    def count(flag):
        return flag.astype(jnp.int32)

    near = count(has_low) + count(has_high)
    pl.semaphore_wait(
        barrier,
        near
        + jnp.where(even, near, 0)
        + 1
        + count(both(odd, t < slices - 1))
        + count(seeds)
        + count(goes_on)
        + 2 * count(far)
        + count(helps),
    )

    def z_half(side, c):
        at_row = FINE - BLOCK - BLOCK * c if side == 0 else FINE + ROWS + BLOCK * c
        return zone.at[pl.ds(at_row, BLOCK)]

    def z_copy(side, tm, space):
        source = FINE + BLOCK - BLOCK * core if side == 0 else FINE + BLOCK * core
        return remote(
            zone.at[pl.ds(source, BLOCK)],
            z_half(side, core),
            z_send.at[side],
            z_recv.at[side],
            at(tm, space),
        )

    def z_mate(side):
        return remote(
            z_half(side, core), z_half(side, core), zm_send.at[side], zm_recv.at[side], at(mate, s)
        )

    def z_mate_wait(side):
        part = z_half(side, 1 - core)
        remote(part, part, zm_send.at[side], zm_recv.at[side], at(mate, s)).wait_recv()

    def z_next(side):
        part = z_half(side, core)
        return remote(part, part, zf_send, z_recv.at[side], at(next_t, s))

    def each_zone_copy(act):
        @pl.when(both(has_high, jnp.logical_not(far_high)))
        def _():
            act(z_copy(0, t, s + 1))

        @pl.when(both(has_low, jnp.logical_not(far_low)))
        def _():
            act(z_copy(1, t, s - 1))

        @pl.when(both(far_high, end_chip))
        def _():
            act(z_copy(0, across, s + 1))

        @pl.when(both(far_low, end_chip))
        def _():
            act(z_copy(1, across, s - 1))

    def u_rows(start_row, rows):
        return u.at[0, pl.ds(PAD + start_row, rows)]

    def u_copy(side, batch):
        if side == 0:
            source, to, space = BLOCK - BLOCK * batch, -BLOCK - BLOCK * batch, s + 1
        else:
            source, to, space = BLOCK * batch, ROWS + BLOCK * batch, s - 1
        return remote(
            first.at[pl.ds(source, BLOCK)],
            u_rows(to, BLOCK),
            u_send.at[side, batch],
            u_recv.at[side, batch],
            at(t, space),
        )

    pieces = ((0, 0, 4, -1), (0, 4, 2, 0), (0, 6, 2, 1), (1, 8, 2, -1), (1, 10, 3, 0), (1, 13, 3, 1))

    def piece_copy(side, number):
        batch, skip, rows, helper = pieces[number]
        source = ROWS - skip - rows if side == 0 else skip
        to = -skip - rows if side == 0 else ROWS + skip
        if helper < 0:
            dst, recv, space = u_rows(to, rows), u_recv.at[side, batch], half if side == 0 else half - 1
        else:
            dst, recv = rbuf.at[pl.ds(2 * batch, rows)], r_recv.at[batch]
            space = (
                (half - 5, half - 13)[helper] if side == 0 else (half + 4, half + 12)[helper]
            )
        return remote(first.at[pl.ds(source, rows)], dst, r_send.at[number], recv, at(t, space))

    def forward_copy(side, number):
        batch, skip, rows, helper = pieces[number]
        to = -skip - rows if side == 0 else ROWS + skip
        return remote(
            rbuf.at[pl.ds(2 * batch, rows)],
            u_rows(to, rows),
            f_send.at[batch],
            u_recv.at[side, batch],
            at(t, half if side == 0 else half - 1),
        )

    def each_piece(act):
        for side, flag in ((0, far_high), (1, far_low)):

            @pl.when(flag)
            def _():
                for number in (1, 2, 0, 4, 5, 3):
                    act(piece_copy(side, number))

    def each_forward(act):
        for side, flags in ((0, low_helper), (1, high_helper)):
            for helper in range(2):

                @pl.when(flags[helper])
                def _():
                    for number in range(len(pieces)):
                        if pieces[number][3] == helper:
                            act(side, number)

    def each_state_copy(batch, act):
        @pl.when(both(has_high, jnp.logical_not(far_high)))
        def _():
            act(u_copy(0, batch))

        @pl.when(both(has_low, jnp.logical_not(far_low)))
        def _():
            act(u_copy(1, batch))

    start = lambda copy: copy.start()
    sent = lambda copy: copy.wait_send()
    each_zone_copy(start)
    each_piece(start)
    each_state_copy(0, start)
    each_state_copy(1, start)

    numbers = []
    for q in range(ZONES):
        v = zv[q]
        numbers.append((cond[q], xv[v], cv[1, v], cv[0, v]))
    zi, li = iotas((NZ, LANES))

    def weights(x, carry):
        for tile in range(TILES):
            sl = slice(tile * LANES, (tile + 1) * LANES)
            z = zone[FINE + x, :, sl].astype(jnp.int32)
            bits = [(z & (1 << b)) != 0 for b in range(4)]
            found = []
            for n in range(4):
                level = [numbers[q][n] for q in range(ZONES)]
                for b in range(4):
                    level = [
                        jnp.where(bits[b], level[2 * j + 1], level[2 * j])
                        for j in range(len(level) // 2)
                    ]
                found.append(level[0])
            d, cx, cz, cy = found
            xm = d + jnp.maximum(cx, 0.0)
            xp = d - jnp.minimum(cx, 0.0)
            zm = d + jnp.maximum(cz, 0.0)
            zp = d - jnp.minimum(cz, 0.0)
            ym = d + jnp.maximum(cy, 0.0)
            yp = d - jnp.minimum(cy, 0.0)
            w[0, PAD + x, :, sl] = 1.0 - (((xm + xp) + (zm + zp)) + (ym + yp))
            w[1, PAD + x, :, sl] = xm
            w[2, PAD + x, :, sl] = xp
            w[3, PAD + x, :, sl] = jnp.where(zi == 0, 0.0, zm)
            w[4, PAD + x, :, sl] = jnp.where(zi == NZ - 1, 0.0, zp)
            if tile == 0:
                ym = jnp.where(li == 0, 0.0, ym)
            if tile == TILES - 1:
                yp = jnp.where(li == LANES - 1, 0.0, yp)
            w[5, PAD + x, :, sl] = ym
            w[6, PAD + x, :, sl] = yp
        return carry

    lax.fori_loop(0, ROWS, weights, 0)

    def start_coarse(x):
        gs[x] = coarse_row(u.at[0], PAD + x, ck)

    def two_coarse(n, carry):
        start_coarse(2 * n + 1)
        start_coarse(2 * n + 2)
        return carry

    lax.fori_loop(0, ROWS // 2 - 1, two_coarse, 0)

    def forward(side, number):
        piece_copy(side, number).wait_recv()
        forward_copy(side, number).start()

    each_forward(forward)

    for side, flag, is_far in ((0, has_low, far_low), (1, has_high, far_high)):

        @pl.when(flag)
        def _():
            z_copy(side, t, s).wait_recv()
            z_mate(side).start()

            @pl.when(both(is_far, goes_on))
            def _():
                z_next(side).start()

    for side, flag in ((0, has_low), (1, has_high)):

        @pl.when(flag)
        def _():
            z_mate_wait(side)
            lax.fori_loop(-FINE if side == 0 else ROWS, 0 if side == 0 else ROWS + FINE, weights, 0)

    def state_wait(side, batch):
        u_copy(side, batch).wait_recv()

    @pl.when(both(ascending, has_low))
    def _():
        state_wait(0, 0)
        state_wait(0, 1)

    @pl.when(both(jnp.logical_not(ascending), has_high))
    def _():
        state_wait(1, 0)
        state_wait(1, 1)

    @pl.when(ascending)
    def _():
        start_coarse(0)

    @pl.when(jnp.logical_not(ascending))
    def _():
        start_coarse(ROWS - 1)

    def block(src, dst, x0):
        base = PAD + jnp.where(ascending, x0, ROWS - BLOCK - x0)
        rows = [
            [src[base + r - 1, :, j * LANES : (j + 1) * LANES] for j in range(TILES)]
            for r in range(BLOCK + 2)
        ]
        for r in range(BLOCK):
            x = base + r
            v = rows[r + 1]
            low = [pltpu.roll(v[TILES - 1], 1, 1)] + v[:-1]
            high = v[1:] + [pltpu.roll(v[0], LANES - 1, 1)]
            for j in range(TILES):
                sl = slice(j * LANES, (j + 1) * LANES)
                centre = w[0, x, :, sl] * v[j]
                along_x = w[1, x, :, sl] * rows[r][j] + w[2, x, :, sl] * rows[r + 2][j]
                along_y = w[5, x, :, sl] * low[j] + w[6, x, :, sl] * high[j]
                along_z = w[3, x, :, sl] * pltpu.roll(v[j], 1, 0) + w[4, x, :, sl] * pltpu.roll(
                    v[j], NZ - 1, 0
                )
                dst[x, :, sl] = (centre + along_x) + (along_y + along_z)

    def wedge(n, carry):
        for src, dst, level in ((u.at[0], u.at[1], 2 * n + 1), (u.at[1], u.at[0], 2 * n + 2)):

            def blocks(m, c):
                block(src, dst, ROWS - level - BLOCK * m)
                return c

            lax.fori_loop(1, (2 * (FINE - level) + 7) // BLOCK + 1, blocks, 0)
        return carry

    lax.fori_loop(0, FINE // 2, wedge, 0)

    def slab(x0):
        def pair(n, carry):
            block(u.at[0], u.at[1], x0 - 2 * n - 1)
            block(u.at[1], u.at[0], x0 - 2 * n - 2)
            return carry

        lax.fori_loop(0, FINE // 2, pair, 0)

    @pl.when(ascending)
    def _():
        state_wait(1, 0)
        start_coarse(ROWS - 1)

    @pl.when(jnp.logical_not(ascending))
    def _():
        state_wait(0, 0)
        start_coarse(0)

    slab(ROWS)

    @pl.when(ascending)
    def _():
        state_wait(1, 1)

    @pl.when(jnp.logical_not(ascending))
    def _():
        state_wait(0, 1)

    slab(ROWS + BLOCK)

    keep = jnp.where(t == 0, 0.0, 1.0).astype(jnp.float32)
    depth = slices - 1 - 2 * chip

    def jump(x):
        return u[0, PAD + x] - keep * gs[x]

    def jump_loop(buf):
        def row(x, carry):
            buf[FINE + x] = jump(x)
            return carry

        lax.fori_loop(0, ROWS, row, 0)

    @pl.when(even)
    def _():
        jump_loop(ja)

    @pl.when(odd)
    def _():
        jump_loop(jb)

    def j_mate():
        part = ja.at[pl.ds(FINE, ROWS)]
        return remote(part, part, jm_send, jm_recv, at(mate, s))

    def j_copy(x, up, on_even):
        buf = ja if on_even else jb
        send, recv = (ja_send, ja_recv) if on_even else (jb_send, jb_recv)
        to = FINE + (x - ROWS if up else x + ROWS)
        return remote(
            buf.at[FINE + x],
            buf.at[to],
            send.at[1 if up else 0, x],
            recv.at[to],
            at(t + 1 if on_even else t, s + 1 if up else s - 1),
        )

    def each_jump_copy(act):
        for on_even, flag, rows in ((True, even, depth), (False, odd, depth - 1)):

            @pl.when(flag)
            def _():
                def row(n, carry):
                    @pl.when(has_high)
                    def _():
                        act(j_copy(ROWS - 1 - n, True, on_even))

                    @pl.when(has_low)
                    def _():
                        act(j_copy(n, False, on_even))

                    return carry

                lax.fori_loop(0, rows, row, 0)

    @pl.when(even)
    def _():
        j_mate().start()

    each_jump_copy(start)

    low_end = jnp.where(has_low, -FINE, 0)
    high_end = jnp.where(has_high, ROWS + FINE - 1, ROWS - 1)
    lo_a = jnp.maximum(-depth, low_end)
    hi_a = jnp.minimum(ROWS - 1 + depth, high_end)
    lo_b = jnp.maximum(1 - depth, low_end)
    hi_b = jnp.minimum(ROWS - 2 + depth, high_end)
    lo_i = jnp.maximum(-depth - 1, low_end)
    hi_i = jnp.minimum(ROWS + depth, high_end)
    passes_on = t < slices - 1
    split = jnp.where(far_high, ROWS - 2 * chip, jnp.where(far_low, 2 * chip, ROWS // 2))
    up_late = jnp.where(far_high, split - lo_a + 1, 0)
    down_late = jnp.where(far_low, hi_a - split + 2, 0)
    up_from = jnp.where(far_high, 0, jnp.where(far_low, 2, 1))
    down_from = jnp.where(far_low, 0, jnp.where(far_high, 2, 1))
    up_steps = up_late + jnp.maximum(hi_a - split, hi_b + 1 - split) + 1
    down_steps = down_late + jnp.maximum(split - 1 - lo_a, split - lo_b) + 1

    def c_copy(x):
        return remote(
            cb.at[FINE + x],
            cin.at[FINE + x],
            c_send.at[FINE + x],
            c_recv.at[FINE + x],
            at(t + 2, s),
        )

    def a_copy(x):
        return remote(ca.at[FINE + x], co.at[x], a_send.at[x], a_recv.at[x], at(mate, s))

    def j_wait(x, on_even):
        buf, recv = (ja, ja_recv) if on_even else (jb, jb_recv)
        remote(
            buf.at[FINE + x],
            buf.at[FINE + x],
            (ja_send if on_even else jb_send).at[0, 0],
            recv.at[FINE + x],
            at(t, s),
        ).wait_recv()

    def within(x, lo, hi):
        return both(x >= lo, x <= hi)

    def outside(x):
        return jnp.logical_or(x < 0, x >= ROWS)

    def in_wait(x):
        @pl.when(both(chip > 0, within(x, lo_i, hi_i)))
        def _():
            c_copy(x).wait_recv()

    def a_row(x):
        @pl.when(outside(x))
        def _():
            j_wait(x, True)

        @pl.when(chip == 0)
        def _():
            ca[FINE + x] = ja[FINE + x]

        @pl.when(chip > 0)
        def _():
            ca[FINE + x] = coarse_row(cin, FINE + x, ck) + ja[FINE + x]

        @pl.when(jnp.logical_not(outside(x)))
        def _():
            a_copy(x).start()

    def b_row(x):
        @pl.when(outside(x))
        def _():
            j_wait(x, False)

        cb[FINE + x] = coarse_row(ca, FINE + x, ck) + jb[FINE + x]

        @pl.when(passes_on)
        def _():
            c_copy(x).start()

    @pl.when(odd)
    def _():
        jm_wait = ja.at[pl.ds(FINE, ROWS)]
        remote(jm_wait, jm_wait, jm_send, jm_recv, at(mate, s)).wait_recv()
        in_wait(split - 1)
        in_wait(split)

        def relay(k, carry):
            up = k - up_late
            down = k - down_late

            @pl.when(both(up >= 0, within(split + up, lo_a, hi_a)))
            def _():
                in_wait(split + up + 1)
                a_row(split + up)

            @pl.when(both(down >= 0, within(split - 1 - down, lo_a, hi_a)))
            def _():
                in_wait(split - 2 - down)
                a_row(split - 1 - down)

            @pl.when(both(up >= up_from, within(split + up - 1, lo_b, hi_b)))
            def _():
                b_row(split + up - 1)

            @pl.when(both(down >= down_from, within(split - down, lo_b, hi_b)))
            def _():
                b_row(split - down)

            return carry

        lax.fori_loop(0, jnp.maximum(up_steps, down_steps), relay, 0)
        co[...] = cb[FINE : FINE + ROWS]

    @pl.when(even)
    def _():
        def wait_a(x, carry):
            a_copy(x).wait_recv()
            return carry

        lax.fori_loop(0, ROWS, wait_a, 0)

    out[...] = lax.dot_general(
        co[...].reshape(ROWS * NZ, NY),
        perm[...],
        (((1,), (1,)), ((), ())),
        precision=HIGH,
        preferred_element_type=jnp.float32,
    ).reshape(1, ROWS, NZ, NY)

    each_zone_copy(sent)
    each_piece(sent)
    each_state_copy(0, sent)
    each_state_copy(1, sent)
    each_forward(lambda side, number: forward_copy(side, number).wait_send())
    for side, flag, is_far in ((0, has_low, far_low), (1, has_high, far_high)):

        @pl.when(flag)
        def _():
            z_mate(side).wait_send()

            @pl.when(both(is_far, goes_on))
            def _():
                z_next(side).wait_send()

    each_jump_copy(sent)

    @pl.when(even)
    def _():
        j_mate().wait_send()

    @pl.when(odd)
    def _():
        def drain_a(x, carry):
            a_copy(x).wait_send()
            return carry

        lax.fori_loop(0, ROWS, drain_a, 0)

        @pl.when(passes_on)
        def _():
            def drain(x, carry):
                c_copy(x).wait_send()
                return carry

            lax.fori_loop(lo_b, hi_b + 1, drain, 0)


def shards(
    starts, zone_map, zone_velocity, conductivity, x_velocity, cross_velocity, coarse_kernel
):
    smem = pl.BlockSpec(memory_space=pltpu.SMEM)
    vmem = pl.BlockSpec(memory_space=pltpu.VMEM)
    field = lambda rows: pltpu.VMEM((rows, NZ, NY), jnp.float32)
    dma = pltpu.SemaphoreType.DMA
    return pl.pallas_call(
        kernel,
        name="parareal",
        out_shape=jax.ShapeDtypeStruct(starts.shape, jnp.float32),
        in_specs=[smem] * 5 + [vmem] * 2,
        out_specs=vmem,
        scratch_shapes=[
            pltpu.VMEM((NY, NY), jnp.float32),
            pltpu.VMEM((2, WIDE, NZ, NY), jnp.float32),
            field(ROWS),
            field(EXT),
            pltpu.VMEM((7, WIDE, NZ, NY), jnp.float32),
            field(ROWS),
            field(EXT),
            field(EXT),
            field(EXT),
            field(EXT),
            field(EXT),
            field(ROWS),
            field(5),
            dma((2, 2)),
            dma((2, 2)),
            dma((2,)),
            dma((2,)),
            dma((2,)),
            dma((2,)),
            dma,
            dma((6,)),
            dma((2,)),
            dma((2,)),
            dma((2, ROWS)),
            dma((EXT,)),
            dma((2, ROWS)),
            dma((EXT,)),
            dma,
            dma,
            dma((EXT,)),
            dma((EXT,)),
            dma((ROWS,)),
            dma((ROWS,)),
        ],
        compiler_params=pltpu.CompilerParams(
            collective_id=0, has_side_effects=True, vmem_limit_bytes=56 * 2**20
        ),
    )(
        zone_velocity, conductivity, x_velocity, cross_velocity, coarse_kernel, starts, zone_map
    )


def solution(mesh):
    in_specs = (P("tm", "space", None, None), P("space", None, None), P(), P(), P(), P(), P())
    out_specs = P("tm", "space", None, None)
    return jax.shard_map(shards, mesh=mesh, in_specs=in_specs, out_specs=out_specs, check_vma=False)
```

```python
import functools

import jax
import jax.numpy as jnp
from jax import lax
from jax.experimental import pallas as pl
from jax.experimental.pallas import tpu as pltpu
from jax.sharding import PartitionSpec as P

FINE = 16
ZONES = 16
ROWS = 16
NZ = 16
NY = 512
TILES = 4
LANES = 128
EXT = ROWS + 2 * FINE
BLOCK = 8
PIECE = 2
PAD = 24
WIDE = ROWS + 2 * PAD
MESH = pl.DeviceIdType.MESH
HIGH = lax.Precision.HIGHEST


def iotas(shape):
    return lax.broadcasted_iota(jnp.int32, shape, 0), lax.broadcasted_iota(jnp.int32, shape, 1)


def shift_down(v):
    return jnp.concatenate([pltpu.roll(v[:, NY - LANES :], 1, 1), v[:, : NY - LANES]], axis=1)


def shift_up(v):
    return jnp.concatenate([v[:, LANES:], pltpu.roll(v[:, :LANES], LANES - 1, 1)], axis=1)


def coarse_row(src, x, ck):
    zi, li = iotas((NZ, LANES))
    sums = [[], [], []]
    for tile in range(TILES):
        part = [None] * 3
        for a in range(3):
            v = src[x + a - 1, :, tile * LANES : (tile + 1) * LANES]
            below = jnp.where(zi == 0, 0.0, pltpu.roll(v, 1, 0))
            above = jnp.where(zi == NZ - 1, 0.0, pltpu.roll(v, NZ - 1, 0))
            for b, w in enumerate((below, v, above)):
                for c in range(3):
                    term = ck[a, b, c] * w
                    part[c] = term if part[c] is None else part[c] + term
        for c in range(3):
            sums[c].append(part[c])
    low = [jnp.where(li == 0, 0.0, pltpu.roll(sums[0][TILES - 1], 1, 1))] + sums[0][:-1]
    high = sums[2][1:] + [jnp.where(li == LANES - 1, 0.0, pltpu.roll(sums[2][0], LANES - 1, 1))]
    return jnp.concatenate([low[j] + sums[1][j] + high[j] for j in range(TILES)], axis=1)


def kernel(
    zv, cond, xv, cv, ck, starts, zmap, out,
    perm, u, first, zone, w, gs, ja, jb, cin, ca, cb, co, rbuf,
    u_send, u_recv, z_send, z_recv, zm_send, zm_recv, zf_send, r_send, r_recv, f_send,
    ja_send, ja_recv, jb_send, jb_recv, jm_send, jm_recv, c_send, c_recv, a_send, a_recv,
):
    t = lax.axis_index("tm")
    s = lax.axis_index("space")
    slices = lax.axis_size("tm")
    parts = lax.axis_size("space")
    chips = slices // 2
    chip = t // 2
    core = lax.rem(t, 2)
    odd = core == 1
    even = core == 0
    has_low = s > 0
    has_high = s < parts - 1
    mate = t + 1 - 2 * core
    half = parts // 2
    far_low = s == half
    far_high = s == half - 1
    far = jnp.logical_or(far_low, far_high)
    over = jnp.where(far_low, s - 1, s + 1)
    ascending = s < half
    end_chip = jnp.logical_or(chip == 0, chip == chips - 1)
    seeds = jnp.logical_and(far, end_chip)
    across = 2 * (chips - 1 - chip) + core
    goes_on = jnp.logical_and(
        far, jnp.logical_and(chip != chips // 2 - 1, chip != chips // 2)
    )
    next_t = jnp.where(chip < chips // 2, t + 2, t - 2)
    last_t = jnp.where(chip < chips // 2, t - 2, t + 2)
    helpers = ((half - 4, half - 13, half - 12, half - 15), (half + 3, half + 12, half + 11, half + 14))

    def any_of(flags):
        return functools.reduce(jnp.logical_or, flags)

    helps_up = any_of([s == h for h in helpers[0]])
    helps_down = any_of([s == h for h in helpers[1]])

    def at(tm, space):
        return {"tm": tm, "space": space}

    def both(a, b):
        return jnp.logical_and(a, b)

    def remote(src, dst, send, recv, device):
        return pltpu.make_async_remote_copy(
            src_ref=src,
            dst_ref=dst,
            send_sem=send,
            recv_sem=recv,
            device_id=device,
            device_id_type=MESH,
        )

    barrier = pltpu.get_barrier_semaphore()

    def greet(tm, space):
        pl.semaphore_signal(barrier, inc=1, device_id=at(tm, space), device_id_type=MESH)

    @pl.when(far)
    def _():
        @pl.when(end_chip)
        def _():
            greet(across, over)

        @pl.when(jnp.logical_not(end_chip))
        def _():
            greet(last_t, s)

    @pl.when(jnp.logical_or(helps_up, helps_down))
    def _():
        greet(t, jnp.where(helps_up, half - 1, half))

    @pl.when(has_low)
    def _():
        greet(t, s - 1)

    @pl.when(has_high)
    def _():
        greet(t, s + 1)

    @pl.when(both(odd, has_low))
    def _():
        greet(t - 1, s - 1)

    @pl.when(both(odd, has_high))
    def _():
        greet(t - 1, s + 1)

    greet(mate, s)

    @pl.when(both(odd, t >= 3))
    def _():
        greet(t - 2, s)

    yi, pi = iotas((NY, NY))
    perm[...] = jnp.where(yi == TILES * lax.rem(pi, LANES) + pi // LANES, 1.0, 0.0)
    own = starts[0].reshape(ROWS * NZ, NY)
    zone[FINE : FINE + ROWS] = jnp.dot(
        zmap[...].reshape(ROWS * NZ, NY).astype(jnp.float32),
        perm[...],
        preferred_element_type=jnp.float32,
    ).reshape(ROWS, NZ, NY)
    initial = jnp.dot(
        own, perm[...], precision=HIGH, preferred_element_type=jnp.float32
    ).reshape(ROWS, NZ, NY)
    u[0, PAD : PAD + ROWS] = initial
    first[...] = initial

    zero_row = jnp.zeros((NZ, NY), jnp.float32)

    def clear(begin, edge):
        cin[edge] = zero_row
        ca[edge] = zero_row

        def row(x, carry):
            u[0, x] = zero_row
            u[1, x] = zero_row
            for n in range(7):
                w[n, x] = zero_row
            return carry

        lax.fori_loop(begin, begin + PAD - 4, row, 0)

    @pl.when(jnp.logical_not(has_low))
    def _():
        clear(4, FINE - 1)

    @pl.when(jnp.logical_not(has_high))
    def _():
        clear(PAD + ROWS, FINE + ROWS)

    def count(flag):
        return flag.astype(jnp.int32)

    near = count(has_low) + count(has_high)
    pl.semaphore_wait(
        barrier,
        near
        + jnp.where(even, near, 0)
        + 1
        + count(both(odd, t < slices - 1))
        + count(seeds)
        + count(goes_on)
        + len(helpers[0]) * count(far),
    )

    def z_half(side, c):
        at_row = FINE - BLOCK - BLOCK * c if side == 0 else FINE + ROWS + BLOCK * c
        return zone.at[pl.ds(at_row, BLOCK)]

    def z_copy(side, tm, space, part):
        source = FINE + BLOCK - BLOCK * core if side == 0 else FINE + BLOCK * core
        return remote(
            zone.at[pl.ds(source + PIECE * part, PIECE)],
            z_half(side, core).at[pl.ds(PIECE * part, PIECE)],
            z_send.at[side, part],
            z_recv.at[side, part],
            at(tm, space),
        )

    def z_mate(side):
        return remote(
            z_half(side, core), z_half(side, core), zm_send.at[side], zm_recv.at[side], at(mate, s)
        )

    def z_mate_wait(side):
        part = z_half(side, 1 - core)
        remote(part, part, zm_send.at[side], zm_recv.at[side], at(mate, s)).wait_recv()

    def z_next(side, part):
        rows = z_half(side, core).at[pl.ds(PIECE * part, PIECE)]
        return remote(rows, rows, zf_send.at[part], z_recv.at[side, part], at(next_t, s))

    def each_zone_copy(act):
        @pl.when(both(far_high, end_chip))
        def _():
            for part in range(BLOCK // PIECE):
                act(z_copy(0, across, s + 1, part))

        @pl.when(both(far_low, end_chip))
        def _():
            for part in range(BLOCK // PIECE):
                act(z_copy(1, across, s - 1, part))

        @pl.when(both(has_high, jnp.logical_not(far_high)))
        def _():
            for part in range(BLOCK // PIECE):
                act(z_copy(0, t, s + 1, part))

        @pl.when(both(has_low, jnp.logical_not(far_low)))
        def _():
            for part in range(BLOCK // PIECE):
                act(z_copy(1, t, s - 1, part))

    def u_rows(start_row, rows):
        return u.at[0, pl.ds(PAD + start_row, rows)]

    def u_copy(side, batch):
        if side == 0:
            source, to, space = BLOCK - BLOCK * batch, -BLOCK - BLOCK * batch, s + 1
        else:
            source, to, space = BLOCK * batch, ROWS + BLOCK * batch, s - 1
        return remote(
            first.at[pl.ds(source, BLOCK)],
            u_rows(to, BLOCK),
            u_send.at[side, batch],
            u_recv.at[side, batch],
            at(t, space),
        )

    pieces = (
        (0, 2, 2, 0),
        (0, 4, 1, 1),
        (0, 5, 2, 2),
        (0, 7, 1, 3),
        (0, 0, 2, -1),
        (1, 9, 2, 0),
        (1, 11, 2, 1),
        (1, 13, 1, 2),
        (1, 14, 2, 3),
        (1, 8, 1, -1),
    )

    def piece_copy(side, number):
        batch, skip, rows, helper = pieces[number]
        source = ROWS - skip - rows if side == 0 else skip
        to = -skip - rows if side == 0 else ROWS + skip
        if helper < 0:
            dst, recv, space = u_rows(to, rows), u_recv.at[side, batch], half if side == 0 else half - 1
        else:
            dst, recv = rbuf.at[pl.ds(2 * batch, rows)], r_recv.at[batch]
            space = helpers[side][helper]
        return remote(first.at[pl.ds(source, rows)], dst, r_send.at[number], recv, at(t, space))

    def forward_copy(side, number):
        batch, skip, rows, helper = pieces[number]
        to = -skip - rows if side == 0 else ROWS + skip
        return remote(
            rbuf.at[pl.ds(2 * batch, rows)],
            u_rows(to, rows),
            f_send.at[batch],
            u_recv.at[side, batch],
            at(t, half if side == 0 else half - 1),
        )

    def each_piece(act):
        for side, flag in ((0, far_high), (1, far_low)):

            @pl.when(flag)
            def _():
                for number in range(len(pieces)):
                    act(piece_copy(side, number))

    def each_forward(side, act):
        for helper, space in enumerate(helpers[side]):

            @pl.when(s == space)
            def _():
                for number in range(len(pieces)):
                    if pieces[number][3] == helper:
                        act(side, number)

    def each_state_copy(batch, act):
        @pl.when(both(has_high, jnp.logical_not(far_high)))
        def _():
            act(u_copy(0, batch))

        @pl.when(both(has_low, jnp.logical_not(far_low)))
        def _():
            act(u_copy(1, batch))

    start = lambda copy: copy.start()
    sent = lambda copy: copy.wait_send()
    each_zone_copy(start)
    each_piece(start)
    each_state_copy(0, start)
    each_state_copy(1, start)

    numbers = []
    for q in range(ZONES):
        v = zv[q]
        numbers.append((cond[q], xv[v], cv[1, v], cv[0, v]))
    zi, li = iotas((NZ, LANES))

    def weights(x, carry):
        for tile in range(TILES):
            sl = slice(tile * LANES, (tile + 1) * LANES)
            z = zone[FINE + x, :, sl].astype(jnp.int32)
            bits = [(z & (1 << b)) != 0 for b in range(4)]
            found = []
            for n in range(4):
                level = [numbers[q][n] for q in range(ZONES)]
                for b in range(4):
                    level = [
                        jnp.where(bits[b], level[2 * j + 1], level[2 * j])
                        for j in range(len(level) // 2)
                    ]
                found.append(level[0])
            d, cx, cz, cy = found
            xm = d + jnp.maximum(cx, 0.0)
            xp = d - jnp.minimum(cx, 0.0)
            zm = d + jnp.maximum(cz, 0.0)
            zp = d - jnp.minimum(cz, 0.0)
            ym = d + jnp.maximum(cy, 0.0)
            yp = d - jnp.minimum(cy, 0.0)
            w[0, PAD + x, :, sl] = 1.0 - (((xm + xp) + (zm + zp)) + (ym + yp))
            w[1, PAD + x, :, sl] = xm
            w[2, PAD + x, :, sl] = xp
            w[3, PAD + x, :, sl] = jnp.where(zi == 0, 0.0, zm)
            w[4, PAD + x, :, sl] = jnp.where(zi == NZ - 1, 0.0, zp)
            if tile == 0:
                ym = jnp.where(li == 0, 0.0, ym)
            if tile == TILES - 1:
                yp = jnp.where(li == LANES - 1, 0.0, yp)
            w[5, PAD + x, :, sl] = ym
            w[6, PAD + x, :, sl] = yp
        return carry

    lax.fori_loop(0, ROWS, weights, 0)

    def start_coarse(x):
        gs[x] = coarse_row(u.at[0], PAD + x, ck)

    def two_coarse(n, carry):
        start_coarse(2 * n + 1)
        start_coarse(2 * n + 2)
        return carry

    lax.fori_loop(0, ROWS // 2 - 1, two_coarse, 0)

    def forward(side, number):
        piece_copy(side, number).wait_recv()
        forward_copy(side, number).start()

    each_forward(1, forward)

    sides = ((0, has_low, far_low), (1, has_high, far_high))

    def take_zones(side, hand_on):
        for part in range(BLOCK // PIECE):
            z_copy(side, t, s, part).wait_recv()

            @pl.when(hand_on)
            def _():
                z_next(side, part).start()

        z_mate(side).start()

    def side_weights(side):
        z_mate_wait(side)
        lax.fori_loop(-FINE if side == 0 else ROWS, 0 if side == 0 else ROWS + FINE, weights, 0)

    for side, flag, is_far in sides:

        @pl.when(both(flag, jnp.logical_not(is_far)))
        def _():
            take_zones(side, False)

    for side, flag, is_far in sides:

        @pl.when(both(flag, jnp.logical_not(is_far)))
        def _():
            side_weights(side)

    for side, flag, is_far in sides:

        @pl.when(both(is_far, goes_on))
        def _():
            take_zones(side, True)

    each_forward(0, forward)

    def state_wait(side, batch):
        u_copy(side, batch).wait_recv()

    @pl.when(both(ascending, has_low))
    def _():
        state_wait(0, 0)
        state_wait(0, 1)

    @pl.when(both(jnp.logical_not(ascending), has_high))
    def _():
        state_wait(1, 0)
        state_wait(1, 1)

    @pl.when(ascending)
    def _():
        start_coarse(0)

    @pl.when(jnp.logical_not(ascending))
    def _():
        start_coarse(ROWS - 1)

    def block(src, dst, x0):
        base = PAD + jnp.where(ascending, x0, ROWS - BLOCK - x0)
        rows = [
            [src[base + r - 1, :, j * LANES : (j + 1) * LANES] for j in range(TILES)]
            for r in range(BLOCK + 2)
        ]
        for r in range(BLOCK):
            x = base + r
            v = rows[r + 1]
            low = [pltpu.roll(v[TILES - 1], 1, 1)] + v[:-1]
            high = v[1:] + [pltpu.roll(v[0], LANES - 1, 1)]
            for j in range(TILES):
                sl = slice(j * LANES, (j + 1) * LANES)
                centre = w[0, x, :, sl] * v[j]
                along_x = w[1, x, :, sl] * rows[r][j] + w[2, x, :, sl] * rows[r + 2][j]
                along_y = w[5, x, :, sl] * low[j] + w[6, x, :, sl] * high[j]
                along_z = w[3, x, :, sl] * pltpu.roll(v[j], 1, 0) + w[4, x, :, sl] * pltpu.roll(
                    v[j], NZ - 1, 0
                )
                dst[x, :, sl] = (centre + along_x) + (along_y + along_z)

    def wedge(n, carry):
        for src, dst, level in ((u.at[0], u.at[1], 2 * n + 1), (u.at[1], u.at[0], 2 * n + 2)):

            def blocks(m, c):
                block(src, dst, ROWS - level - BLOCK * m)
                return c

            lax.fori_loop(1, (2 * (FINE - level) + 7) // BLOCK + 1, blocks, 0)
        return carry

    lax.fori_loop(0, FINE // 2, wedge, 0)

    def slab(x0):
        def pair(n, carry):
            block(u.at[0], u.at[1], x0 - 2 * n - 1)
            block(u.at[1], u.at[0], x0 - 2 * n - 2)
            return carry

        lax.fori_loop(0, FINE // 2, pair, 0)

    for side, flag, is_far in sides:

        @pl.when(both(is_far, jnp.logical_not(goes_on)))
        def _():
            take_zones(side, False)

        @pl.when(is_far)
        def _():
            side_weights(side)

    @pl.when(ascending)
    def _():
        state_wait(1, 0)
        start_coarse(ROWS - 1)

    @pl.when(jnp.logical_not(ascending))
    def _():
        state_wait(0, 0)
        start_coarse(0)

    slab(ROWS)

    @pl.when(ascending)
    def _():
        state_wait(1, 1)

    @pl.when(jnp.logical_not(ascending))
    def _():
        state_wait(0, 1)

    slab(ROWS + BLOCK)

    keep = jnp.where(t == 0, 0.0, 1.0).astype(jnp.float32)
    depth = slices - 1 - 2 * chip

    def jump(x):
        return u[0, PAD + x] - keep * gs[x]

    def jump_loop(buf):
        def row(x, carry):
            buf[FINE + x] = jump(x)
            return carry

        lax.fori_loop(0, ROWS, row, 0)

    @pl.when(even)
    def _():
        jump_loop(ja)

    @pl.when(odd)
    def _():
        jump_loop(jb)

    def j_mate():
        part = ja.at[pl.ds(FINE, ROWS)]
        return remote(part, part, jm_send, jm_recv, at(mate, s))

    def j_copy(x, up, on_even):
        buf = ja if on_even else jb
        send, recv = (ja_send, ja_recv) if on_even else (jb_send, jb_recv)
        to = FINE + (x - ROWS if up else x + ROWS)
        return remote(
            buf.at[FINE + x],
            buf.at[to],
            send.at[1 if up else 0, x],
            recv.at[to],
            at(t + 1 if on_even else t, s + 1 if up else s - 1),
        )

    def each_jump_copy(act):
        for on_even, flag, rows in ((True, even, depth), (False, odd, depth - 1)):

            @pl.when(flag)
            def _():
                def row(n, carry):
                    @pl.when(has_high)
                    def _():
                        act(j_copy(ROWS - 1 - n, True, on_even))

                    @pl.when(has_low)
                    def _():
                        act(j_copy(n, False, on_even))

                    return carry

                lax.fori_loop(0, rows, row, 0)

    @pl.when(even)
    def _():
        j_mate().start()

    each_jump_copy(start)

    low_end = jnp.where(has_low, -FINE, 0)
    high_end = jnp.where(has_high, ROWS + FINE - 1, ROWS - 1)
    lo_a = jnp.maximum(-depth, low_end)
    hi_a = jnp.minimum(ROWS - 1 + depth, high_end)
    lo_b = jnp.maximum(1 - depth, low_end)
    hi_b = jnp.minimum(ROWS - 2 + depth, high_end)
    lo_i = jnp.maximum(-depth - 1, low_end)
    hi_i = jnp.minimum(ROWS + depth, high_end)
    passes_on = t < slices - 1
    split = jnp.where(far_high, ROWS - 2 * chip, jnp.where(far_low, 2 * chip, ROWS // 2))
    up_late = jnp.where(far_high, split - lo_a + 1, 0)
    down_late = jnp.where(far_low, hi_a - split + 2, 0)
    up_from = jnp.where(far_high, 0, jnp.where(far_low, 2, 1))
    down_from = jnp.where(far_low, 0, jnp.where(far_high, 2, 1))
    up_steps = up_late + jnp.maximum(hi_a - split, hi_b + 1 - split) + 1
    down_steps = down_late + jnp.maximum(split - 1 - lo_a, split - lo_b) + 1

    def c_copy(x):
        return remote(
            cb.at[FINE + x],
            cin.at[FINE + x],
            c_send.at[FINE + x],
            c_recv.at[FINE + x],
            at(t + 2, s),
        )

    def a_copy(x):
        return remote(ca.at[FINE + x], co.at[x], a_send.at[x], a_recv.at[x], at(mate, s))

    def j_wait(x, on_even):
        buf, recv = (ja, ja_recv) if on_even else (jb, jb_recv)
        remote(
            buf.at[FINE + x],
            buf.at[FINE + x],
            (ja_send if on_even else jb_send).at[0, 0],
            recv.at[FINE + x],
            at(t, s),
        ).wait_recv()

    def within(x, lo, hi):
        return both(x >= lo, x <= hi)

    def outside(x):
        return jnp.logical_or(x < 0, x >= ROWS)

    def in_wait(x):
        @pl.when(both(chip > 0, within(x, lo_i, hi_i)))
        def _():
            c_copy(x).wait_recv()

    def a_row(x):
        @pl.when(outside(x))
        def _():
            j_wait(x, True)

        @pl.when(chip == 0)
        def _():
            ca[FINE + x] = ja[FINE + x]

        @pl.when(chip > 0)
        def _():
            ca[FINE + x] = coarse_row(cin, FINE + x, ck) + ja[FINE + x]

        @pl.when(jnp.logical_not(outside(x)))
        def _():
            a_copy(x).start()

    def b_row(x):
        @pl.when(outside(x))
        def _():
            j_wait(x, False)

        cb[FINE + x] = coarse_row(ca, FINE + x, ck) + jb[FINE + x]

        @pl.when(passes_on)
        def _():
            c_copy(x).start()

    @pl.when(odd)
    def _():
        jm_wait = ja.at[pl.ds(FINE, ROWS)]
        remote(jm_wait, jm_wait, jm_send, jm_recv, at(mate, s)).wait_recv()
        in_wait(split - 1)
        in_wait(split)

        def relay(k, carry):
            up = k - up_late
            down = k - down_late

            @pl.when(both(up >= 0, within(split + up, lo_a, hi_a)))
            def _():
                in_wait(split + up + 1)
                a_row(split + up)

            @pl.when(both(down >= 0, within(split - 1 - down, lo_a, hi_a)))
            def _():
                in_wait(split - 2 - down)
                a_row(split - 1 - down)

            @pl.when(both(up >= up_from, within(split + up - 1, lo_b, hi_b)))
            def _():
                b_row(split + up - 1)

            @pl.when(both(down >= down_from, within(split - down, lo_b, hi_b)))
            def _():
                b_row(split - down)

            return carry

        lax.fori_loop(0, jnp.maximum(up_steps, down_steps), relay, 0)
        co[...] = cb[FINE : FINE + ROWS]

    @pl.when(even)
    def _():
        def wait_a(x, carry):
            a_copy(x).wait_recv()
            return carry

        lax.fori_loop(0, ROWS, wait_a, 0)

    out[...] = lax.dot_general(
        co[...].reshape(ROWS * NZ, NY),
        perm[...],
        (((1,), (1,)), ((), ())),
        precision=HIGH,
        preferred_element_type=jnp.float32,
    ).reshape(1, ROWS, NZ, NY)

    each_zone_copy(sent)
    each_piece(sent)
    each_state_copy(0, sent)
    each_state_copy(1, sent)
    for side in range(2):
        each_forward(side, lambda side, number: forward_copy(side, number).wait_send())
    for side, flag, is_far in sides:

        @pl.when(flag)
        def _():
            z_mate(side).wait_send()

            @pl.when(both(is_far, goes_on))
            def _():
                for part in range(BLOCK // PIECE):
                    z_next(side, part).wait_send()

    each_jump_copy(sent)

    @pl.when(even)
    def _():
        j_mate().wait_send()

    @pl.when(odd)
    def _():
        def drain_a(x, carry):
            a_copy(x).wait_send()
            return carry

        lax.fori_loop(0, ROWS, drain_a, 0)

        @pl.when(passes_on)
        def _():
            def drain(x, carry):
                c_copy(x).wait_send()
                return carry

            lax.fori_loop(lo_b, hi_b + 1, drain, 0)


def shards(
    starts, zone_map, zone_velocity, conductivity, x_velocity, cross_velocity, coarse_kernel
):
    smem = pl.BlockSpec(memory_space=pltpu.SMEM)
    vmem = pl.BlockSpec(memory_space=pltpu.VMEM)
    field = lambda rows: pltpu.VMEM((rows, NZ, NY), jnp.float32)
    dma = pltpu.SemaphoreType.DMA
    return pl.pallas_call(
        kernel,
        name="parareal",
        out_shape=jax.ShapeDtypeStruct(starts.shape, jnp.float32),
        in_specs=[smem] * 5 + [vmem] * 2,
        out_specs=vmem,
        scratch_shapes=[
            pltpu.VMEM((NY, NY), jnp.float32),
            pltpu.VMEM((2, WIDE, NZ, NY), jnp.float32),
            field(ROWS),
            field(EXT),
            pltpu.VMEM((7, WIDE, NZ, NY), jnp.float32),
            field(ROWS),
            field(EXT),
            field(EXT),
            field(EXT),
            field(EXT),
            field(EXT),
            field(ROWS),
            field(4),
            dma((2, 2)),
            dma((2, 2)),
            dma((2, BLOCK // PIECE)),
            dma((2, BLOCK // PIECE)),
            dma((2,)),
            dma((2,)),
            dma((BLOCK // PIECE,)),
            dma((10,)),
            dma((2,)),
            dma((2,)),
            dma((2, ROWS)),
            dma((EXT,)),
            dma((2, ROWS)),
            dma((EXT,)),
            dma,
            dma,
            dma((EXT,)),
            dma((EXT,)),
            dma((ROWS,)),
            dma((ROWS,)),
        ],
        compiler_params=pltpu.CompilerParams(
            collective_id=0, has_side_effects=True, vmem_limit_bytes=56 * 2**20
        ),
    )(
        zone_velocity, conductivity, x_velocity, cross_velocity, coarse_kernel, starts, zone_map
    )


def solution(mesh):
    in_specs = (P("tm", "space", None, None), P("space", None, None), P(), P(), P(), P(), P())
    out_specs = P("tm", "space", None, None)
    return jax.shard_map(shards, mesh=mesh, in_specs=in_specs, out_specs=out_specs, check_vma=False)
```

```python
import functools

import jax
import jax.numpy as jnp
from jax import lax
from jax.experimental import pallas as pl
from jax.experimental.pallas import tpu as pltpu
from jax.sharding import PartitionSpec as P

FINE = 16
ZONES = 16
ROWS = 16
NZ = 16
NY = 512
TILES = 4
LANES = 128
EXT = ROWS + 2 * FINE
BLOCK = 8
PIECE = 2
PAD = 24
WIDE = ROWS + 2 * PAD
MESH = pl.DeviceIdType.MESH
HIGH = lax.Precision.HIGHEST


def iotas(shape):
    return lax.broadcasted_iota(jnp.int32, shape, 0), lax.broadcasted_iota(jnp.int32, shape, 1)


def shift_down(v):
    return jnp.concatenate([pltpu.roll(v[:, NY - LANES :], 1, 1), v[:, : NY - LANES]], axis=1)


def shift_up(v):
    return jnp.concatenate([v[:, LANES:], pltpu.roll(v[:, :LANES], LANES - 1, 1)], axis=1)


def coarse_row(src, x, ck):
    zi, li = iotas((NZ, LANES))
    sums = [[], [], []]
    for tile in range(TILES):
        part = [None] * 3
        for a in range(3):
            v = src[x + a - 1, :, tile * LANES : (tile + 1) * LANES]
            below = jnp.where(zi == 0, 0.0, pltpu.roll(v, 1, 0))
            above = jnp.where(zi == NZ - 1, 0.0, pltpu.roll(v, NZ - 1, 0))
            for b, w in enumerate((below, v, above)):
                for c in range(3):
                    term = ck[a, b, c] * w
                    part[c] = term if part[c] is None else part[c] + term
        for c in range(3):
            sums[c].append(part[c])
    low = [jnp.where(li == 0, 0.0, pltpu.roll(sums[0][TILES - 1], 1, 1))] + sums[0][:-1]
    high = sums[2][1:] + [jnp.where(li == LANES - 1, 0.0, pltpu.roll(sums[2][0], LANES - 1, 1))]
    return jnp.concatenate([low[j] + sums[1][j] + high[j] for j in range(TILES)], axis=1)


def kernel(
    zv, cond, xv, cv, ck, starts, zmap, out,
    perm, u, first, zone, w, gs, ja, jb, cin, ca, cb, co, rbuf,
    u_send, u_recv, z_send, z_recv, zm_send, zm_recv, zf_send, r_send, r_recv, f_send,
    ja_send, ja_recv, jb_send, jb_recv, jm_send, jm_recv, c_send, c_recv, a_send, a_recv,
):
    t = lax.axis_index("tm")
    s = lax.axis_index("space")
    slices = lax.axis_size("tm")
    parts = lax.axis_size("space")
    chips = slices // 2
    chip = t // 2
    core = lax.rem(t, 2)
    odd = core == 1
    even = core == 0
    has_low = s > 0
    has_high = s < parts - 1
    mate = t + 1 - 2 * core
    half = parts // 2
    far_low = s == half
    far_high = s == half - 1
    far = jnp.logical_or(far_low, far_high)
    over = jnp.where(far_low, s - 1, s + 1)
    ascending = s < half
    end_chip = jnp.logical_or(chip == 0, chip == chips - 1)
    seeds = jnp.logical_and(far, end_chip)
    across = 2 * (chips - 1 - chip) + core
    goes_on = jnp.logical_and(
        far, jnp.logical_and(chip != chips // 2 - 1, chip != chips // 2)
    )
    next_t = jnp.where(chip < chips // 2, t + 2, t - 2)
    last_t = jnp.where(chip < chips // 2, t - 2, t + 2)
    columns = (half - 4, half - 16, half - 8, half - 13, half - 5)
    helpers = (columns, tuple(parts - 1 - h for h in columns))

    own_column = sum(
        jnp.where(chip == n, h, 0) for n, h in enumerate((half - 12, half - 4, half - 8, half - 15))
    )
    jump_helper = (own_column, parts - 1 - own_column)
    by_column = chip < 4

    def any_of(flags):
        return functools.reduce(jnp.logical_or, flags)

    helps_up = any_of([s == h for h in helpers[0]])
    helps_down = any_of([s == h for h in helpers[1]])

    def at(tm, space):
        return {"tm": tm, "space": space}

    def both(a, b):
        return jnp.logical_and(a, b)

    def remote(src, dst, send, recv, device):
        return pltpu.make_async_remote_copy(
            src_ref=src,
            dst_ref=dst,
            send_sem=send,
            recv_sem=recv,
            device_id=device,
            device_id_type=MESH,
        )

    barrier = pltpu.get_barrier_semaphore()

    def greet(tm, space):
        pl.semaphore_signal(barrier, inc=1, device_id=at(tm, space), device_id_type=MESH)

    @pl.when(far)
    def _():
        @pl.when(end_chip)
        def _():
            greet(across, over)

        @pl.when(jnp.logical_not(end_chip))
        def _():
            greet(last_t, s)

    @pl.when(jnp.logical_or(helps_up, helps_down))
    def _():
        greet(t, jnp.where(helps_up, half - 1, half))

    @pl.when(has_low)
    def _():
        greet(t, s - 1)

    @pl.when(has_high)
    def _():
        greet(t, s + 1)

    @pl.when(both(odd, has_low))
    def _():
        greet(t - 1, s - 1)

    @pl.when(both(odd, has_high))
    def _():
        greet(t - 1, s + 1)

    for side in range(2):

        @pl.when(both(both(even, by_column), s == jump_helper[side]))
        def _():
            greet(t + 1, half - 1 if side == 0 else half)

    greet(mate, s)

    @pl.when(both(odd, t >= 3))
    def _():
        greet(t - 2, s)

    yi, pi = iotas((NY, NY))
    perm[...] = jnp.where(yi == TILES * lax.rem(pi, LANES) + pi // LANES, 1.0, 0.0)
    own = starts[0].reshape(ROWS * NZ, NY)
    zone[FINE : FINE + ROWS] = jnp.dot(
        zmap[...].reshape(ROWS * NZ, NY).astype(jnp.float32),
        perm[...],
        preferred_element_type=jnp.float32,
    ).reshape(ROWS, NZ, NY)
    initial = jnp.dot(
        own, perm[...], precision=HIGH, preferred_element_type=jnp.float32
    ).reshape(ROWS, NZ, NY)
    u[0, PAD : PAD + ROWS] = initial
    first[...] = initial

    zero_row = jnp.zeros((NZ, NY), jnp.float32)

    def clear(begin, edge):
        cin[edge] = zero_row
        ca[edge] = zero_row

        def row(x, carry):
            u[0, x] = zero_row
            u[1, x] = zero_row
            for n in range(7):
                w[n, x] = zero_row
            return carry

        lax.fori_loop(begin, begin + PAD - 4, row, 0)

    @pl.when(jnp.logical_not(has_low))
    def _():
        clear(4, FINE - 1)

    @pl.when(jnp.logical_not(has_high))
    def _():
        clear(PAD + ROWS, FINE + ROWS)

    def count(flag):
        return flag.astype(jnp.int32)

    near = count(has_low) + count(has_high)
    pl.semaphore_wait(
        barrier,
        near
        + jnp.where(even, near, 0)
        + 1
        + count(both(odd, t < slices - 1))
        + count(seeds)
        + count(goes_on)
        + len(helpers[0]) * count(far)
        + count(both(far, both(odd, by_column))),
    )

    def z_half(side, c):
        at_row = FINE - BLOCK - BLOCK * c if side == 0 else FINE + ROWS + BLOCK * c
        return zone.at[pl.ds(at_row, BLOCK)]

    def z_copy(side, tm, space, part):
        source = FINE + BLOCK - BLOCK * core if side == 0 else FINE + BLOCK * core
        return remote(
            zone.at[pl.ds(source + PIECE * part, PIECE)],
            z_half(side, core).at[pl.ds(PIECE * part, PIECE)],
            z_send.at[side, part],
            z_recv.at[side, part],
            at(tm, space),
        )

    def z_mate(side):
        return remote(
            z_half(side, core), z_half(side, core), zm_send.at[side], zm_recv.at[side], at(mate, s)
        )

    def z_mate_wait(side):
        part = z_half(side, 1 - core)
        remote(part, part, zm_send.at[side], zm_recv.at[side], at(mate, s)).wait_recv()

    def z_next(side, part):
        rows = z_half(side, core).at[pl.ds(PIECE * part, PIECE)]
        return remote(rows, rows, zf_send.at[part], z_recv.at[side, part], at(next_t, s))

    def each_zone_copy(act):
        @pl.when(both(far_high, end_chip))
        def _():
            for part in range(BLOCK // PIECE):
                act(z_copy(0, across, s + 1, part))

        @pl.when(both(far_low, end_chip))
        def _():
            for part in range(BLOCK // PIECE):
                act(z_copy(1, across, s - 1, part))

        @pl.when(both(has_high, jnp.logical_not(far_high)))
        def _():
            for part in range(BLOCK // PIECE):
                act(z_copy(0, t, s + 1, part))

        @pl.when(both(has_low, jnp.logical_not(far_low)))
        def _():
            for part in range(BLOCK // PIECE):
                act(z_copy(1, t, s - 1, part))

    def u_rows(start_row, rows):
        return u.at[0, pl.ds(PAD + start_row, rows)]

    def u_copy(side, batch):
        if side == 0:
            source, to, space = BLOCK - BLOCK * batch, -BLOCK - BLOCK * batch, s + 1
        else:
            source, to, space = BLOCK * batch, ROWS + BLOCK * batch, s - 1
        return remote(
            first.at[pl.ds(source, BLOCK)],
            u_rows(to, BLOCK),
            u_send.at[side, batch],
            u_recv.at[side, batch],
            at(t, space),
        )

    pieces = (
        (0, 2, 2, 0),
        (0, 5, 2, 2),
        (0, 4, 1, 1),
        (0, 7, 1, 3),
        (0, 0, 2, -1),
        (1, 9, 2, 0),
        (1, 13, 1, 2),
        (1, 11, 2, 1),
        (1, 15, 1, 4),
        (1, 14, 1, 3),
        (1, 8, 1, -1),
    )

    def piece_copy(side, number):
        batch, skip, rows, helper = pieces[number]
        source = ROWS - skip - rows if side == 0 else skip
        to = -skip - rows if side == 0 else ROWS + skip
        if helper < 0:
            dst, recv, space = u_rows(to, rows), u_recv.at[side, batch], half if side == 0 else half - 1
        else:
            dst, recv = rbuf.at[pl.ds(2 * batch, rows)], r_recv.at[batch]
            space = helpers[side][helper]
        return remote(first.at[pl.ds(source, rows)], dst, r_send.at[number], recv, at(t, space))

    def forward_copy(side, number):
        batch, skip, rows, helper = pieces[number]
        to = -skip - rows if side == 0 else ROWS + skip
        return remote(
            rbuf.at[pl.ds(2 * batch, rows)],
            u_rows(to, rows),
            f_send.at[batch],
            u_recv.at[side, batch],
            at(t, half if side == 0 else half - 1),
        )

    def each_piece(act):
        for side, flag in ((0, far_high), (1, far_low)):

            @pl.when(flag)
            def _():
                for number in range(len(pieces)):
                    act(piece_copy(side, number))

    def each_forward(side, act):
        for helper, space in enumerate(helpers[side]):

            @pl.when(s == space)
            def _():
                for number in range(len(pieces)):
                    if pieces[number][3] == helper:
                        act(side, number)

    def each_state_copy(batch, act):
        @pl.when(both(has_high, jnp.logical_not(far_high)))
        def _():
            act(u_copy(0, batch))

        @pl.when(both(has_low, jnp.logical_not(far_low)))
        def _():
            act(u_copy(1, batch))

    start = lambda copy: copy.start()
    sent = lambda copy: copy.wait_send()
    each_piece(start)
    each_zone_copy(start)
    each_state_copy(0, start)
    each_state_copy(1, start)

    numbers = []
    for q in range(ZONES):
        v = zv[q]
        numbers.append((cond[q], xv[v], cv[1, v], cv[0, v]))
    zi, li = iotas((NZ, LANES))

    def weights(x, carry):
        for tile in range(TILES):
            sl = slice(tile * LANES, (tile + 1) * LANES)
            z = zone[FINE + x, :, sl].astype(jnp.int32)
            bits = [(z & (1 << b)) != 0 for b in range(4)]
            found = []
            for n in range(4):
                level = [numbers[q][n] for q in range(ZONES)]
                for b in range(4):
                    level = [
                        jnp.where(bits[b], level[2 * j + 1], level[2 * j])
                        for j in range(len(level) // 2)
                    ]
                found.append(level[0])
            d, cx, cz, cy = found
            xm = d + jnp.maximum(cx, 0.0)
            xp = d - jnp.minimum(cx, 0.0)
            zm = d + jnp.maximum(cz, 0.0)
            zp = d - jnp.minimum(cz, 0.0)
            ym = d + jnp.maximum(cy, 0.0)
            yp = d - jnp.minimum(cy, 0.0)
            w[0, PAD + x, :, sl] = 1.0 - (((xm + xp) + (zm + zp)) + (ym + yp))
            w[1, PAD + x, :, sl] = xm
            w[2, PAD + x, :, sl] = xp
            w[3, PAD + x, :, sl] = jnp.where(zi == 0, 0.0, zm)
            w[4, PAD + x, :, sl] = jnp.where(zi == NZ - 1, 0.0, zp)
            if tile == 0:
                ym = jnp.where(li == 0, 0.0, ym)
            if tile == TILES - 1:
                yp = jnp.where(li == LANES - 1, 0.0, yp)
            w[5, PAD + x, :, sl] = ym
            w[6, PAD + x, :, sl] = yp
        return carry

    lax.fori_loop(0, ROWS, weights, 0)

    def start_coarse(x):
        gs[x] = coarse_row(u.at[0], PAD + x, ck)

    def two_coarse(n, carry):
        start_coarse(2 * n + 1)
        start_coarse(2 * n + 2)
        return carry

    lax.fori_loop(0, ROWS // 2 - 1, two_coarse, 0)

    def forward(side, number):
        piece_copy(side, number).wait_recv()
        forward_copy(side, number).start()

    each_forward(1, forward)

    sides = ((0, has_low, far_low), (1, has_high, far_high))

    def take_zones(side, hand_on):
        for part in range(BLOCK // PIECE):
            z_copy(side, t, s, part).wait_recv()

            @pl.when(hand_on)
            def _():
                z_next(side, part).start()

        z_mate(side).start()

    def side_weights(side):
        z_mate_wait(side)
        lax.fori_loop(-FINE if side == 0 else ROWS, 0 if side == 0 else ROWS + FINE, weights, 0)

    for side, flag, is_far in sides:

        @pl.when(both(flag, jnp.logical_not(is_far)))
        def _():
            take_zones(side, False)

    for side, flag, is_far in sides:

        @pl.when(both(flag, jnp.logical_not(is_far)))
        def _():
            side_weights(side)

    for side, flag, is_far in sides:

        @pl.when(both(is_far, goes_on))
        def _():
            take_zones(side, True)

    each_forward(0, forward)

    def state_wait(side, batch):
        u_copy(side, batch).wait_recv()

    @pl.when(both(ascending, has_low))
    def _():
        state_wait(0, 0)
        state_wait(0, 1)

    @pl.when(both(jnp.logical_not(ascending), has_high))
    def _():
        state_wait(1, 0)
        state_wait(1, 1)

    @pl.when(ascending)
    def _():
        start_coarse(0)

    @pl.when(jnp.logical_not(ascending))
    def _():
        start_coarse(ROWS - 1)

    def block(src, dst, x0):
        base = PAD + jnp.where(ascending, x0, ROWS - BLOCK - x0)
        rows = [
            [src[base + r - 1, :, j * LANES : (j + 1) * LANES] for j in range(TILES)]
            for r in range(BLOCK + 2)
        ]
        for r in range(BLOCK):
            x = base + r
            v = rows[r + 1]
            low = [pltpu.roll(v[TILES - 1], 1, 1)] + v[:-1]
            high = v[1:] + [pltpu.roll(v[0], LANES - 1, 1)]
            for j in range(TILES):
                sl = slice(j * LANES, (j + 1) * LANES)
                centre = w[0, x, :, sl] * v[j]
                along_x = w[1, x, :, sl] * rows[r][j] + w[2, x, :, sl] * rows[r + 2][j]
                along_y = w[5, x, :, sl] * low[j] + w[6, x, :, sl] * high[j]
                along_z = w[3, x, :, sl] * pltpu.roll(v[j], 1, 0) + w[4, x, :, sl] * pltpu.roll(
                    v[j], NZ - 1, 0
                )
                dst[x, :, sl] = (centre + along_x) + (along_y + along_z)

    def wedge(n, carry):
        for src, dst, level in ((u.at[0], u.at[1], 2 * n + 1), (u.at[1], u.at[0], 2 * n + 2)):

            def blocks(m, c):
                block(src, dst, ROWS - level - BLOCK * m)
                return c

            lax.fori_loop(1, (2 * (FINE - level) + 7) // BLOCK + 1, blocks, 0)
        return carry

    lax.fori_loop(0, FINE // 2, wedge, 0)

    def slab(x0):
        def pair(n, carry):
            block(u.at[0], u.at[1], x0 - 2 * n - 1)
            block(u.at[1], u.at[0], x0 - 2 * n - 2)
            return carry

        lax.fori_loop(0, FINE // 2, pair, 0)

    for side, flag, is_far in sides:

        @pl.when(both(is_far, jnp.logical_not(goes_on)))
        def _():
            take_zones(side, False)

        @pl.when(is_far)
        def _():
            side_weights(side)

    @pl.when(ascending)
    def _():
        state_wait(1, 0)
        start_coarse(ROWS - 1)

    @pl.when(jnp.logical_not(ascending))
    def _():
        state_wait(0, 0)
        start_coarse(0)

    slab(ROWS)

    @pl.when(ascending)
    def _():
        state_wait(1, 1)

    @pl.when(jnp.logical_not(ascending))
    def _():
        state_wait(0, 1)

    slab(ROWS + BLOCK)

    keep = jnp.where(t == 0, 0.0, 1.0).astype(jnp.float32)
    depth = slices - 1 - 2 * chip

    def jump(x):
        return u[0, PAD + x] - keep * gs[x]

    def jump_loop(buf):
        def row(x, carry):
            buf[FINE + x] = jump(x)
            return carry

        lax.fori_loop(0, ROWS, row, 0)

    @pl.when(even)
    def _():
        jump_loop(ja)

    @pl.when(odd)
    def _():
        jump_loop(jb)

    def j_mate():
        part = ja.at[pl.ds(FINE, ROWS)]
        return remote(part, part, jm_send, jm_recv, at(mate, s))

    def j_copy(x, up, on_even):
        buf = ja if on_even else jb
        send, recv = (ja_send, ja_recv) if on_even else (jb_send, jb_recv)
        to = FINE + (x - ROWS if up else x + ROWS)
        if on_even:
            device = at(t + 1, s + 1 if up else s - 1)
        else:
            crosses = both(far_high if up else far_low, by_column)
            device = at(
                jnp.where(crosses, t - 1, t),
                jnp.where(crosses, jump_helper[0 if up else 1], s + 1 if up else s - 1),
            )
        return remote(buf.at[FINE + x], buf.at[to], send.at[1 if up else 0, x], recv.at[to], device)

    def jump_relay(n, up):
        x = ROWS - 1 - n if up else n
        to = FINE + (x - ROWS if up else x + ROWS)
        return remote(
            jb.at[to],
            jb.at[to],
            jb_send.at[1 if up else 0, x],
            jb_recv.at[to],
            at(t + 1, half if up else half - 1),
        )

    def each_jump_relay(act):
        for up in (True, False):

            @pl.when(both(both(even, by_column), s == jump_helper[0 if up else 1]))
            def _():
                def row(n, carry):
                    act(jump_relay(n, up))
                    return carry

                lax.fori_loop(0, depth - 1, row, 0)

    def each_jump_copy(act):
        for on_even, flag, rows in ((True, even, depth), (False, odd, depth - 1)):

            @pl.when(flag)
            def _():
                def row(n, carry):
                    @pl.when(has_high)
                    def _():
                        act(j_copy(ROWS - 1 - n, True, on_even))

                    @pl.when(has_low)
                    def _():
                        act(j_copy(n, False, on_even))

                    return carry

                lax.fori_loop(0, rows, row, 0)

    @pl.when(even)
    def _():
        j_mate().start()

    each_jump_copy(start)

    def relay_jump(copy):
        copy.wait_recv()
        copy.start()

    each_jump_relay(relay_jump)

    low_end = jnp.where(has_low, -FINE, 0)
    high_end = jnp.where(has_high, ROWS + FINE - 1, ROWS - 1)
    lo_a = jnp.maximum(-depth, low_end)
    hi_a = jnp.minimum(ROWS - 1 + depth, high_end)
    lo_b = jnp.maximum(1 - depth, low_end)
    hi_b = jnp.minimum(ROWS - 2 + depth, high_end)
    lo_i = jnp.maximum(-depth - 1, low_end)
    hi_i = jnp.minimum(ROWS + depth, high_end)
    passes_on = t < slices - 1
    split = jnp.where(far_high, ROWS - 2 * chip, jnp.where(far_low, 2 * chip, ROWS // 2))
    up_late = jnp.where(far_high, split - lo_a + 1, 0)
    down_late = jnp.where(far_low, hi_a - split + 2, 0)
    up_from = jnp.where(far_high, 0, jnp.where(far_low, 2, 1))
    down_from = jnp.where(far_low, 0, jnp.where(far_high, 2, 1))
    up_steps = up_late + jnp.maximum(hi_a - split, hi_b + 1 - split) + 1
    down_steps = down_late + jnp.maximum(split - 1 - lo_a, split - lo_b) + 1

    def c_copy(x):
        return remote(
            cb.at[FINE + x],
            cin.at[FINE + x],
            c_send.at[FINE + x],
            c_recv.at[FINE + x],
            at(t + 2, s),
        )

    def a_copy(x):
        return remote(ca.at[FINE + x], co.at[x], a_send.at[x], a_recv.at[x], at(mate, s))

    def j_wait(x, on_even):
        buf, recv = (ja, ja_recv) if on_even else (jb, jb_recv)
        remote(
            buf.at[FINE + x],
            buf.at[FINE + x],
            (ja_send if on_even else jb_send).at[0, 0],
            recv.at[FINE + x],
            at(t, s),
        ).wait_recv()

    def within(x, lo, hi):
        return both(x >= lo, x <= hi)

    def outside(x):
        return jnp.logical_or(x < 0, x >= ROWS)

    def in_wait(x):
        @pl.when(both(chip > 0, within(x, lo_i, hi_i)))
        def _():
            c_copy(x).wait_recv()

    def a_row(x):
        @pl.when(outside(x))
        def _():
            j_wait(x, True)

        @pl.when(chip == 0)
        def _():
            ca[FINE + x] = ja[FINE + x]

        @pl.when(chip > 0)
        def _():
            ca[FINE + x] = coarse_row(cin, FINE + x, ck) + ja[FINE + x]

        @pl.when(jnp.logical_not(outside(x)))
        def _():
            a_copy(x).start()

    def b_row(x):
        @pl.when(outside(x))
        def _():
            j_wait(x, False)

        cb[FINE + x] = coarse_row(ca, FINE + x, ck) + jb[FINE + x]

        @pl.when(passes_on)
        def _():
            c_copy(x).start()

    @pl.when(odd)
    def _():
        jm_wait = ja.at[pl.ds(FINE, ROWS)]
        remote(jm_wait, jm_wait, jm_send, jm_recv, at(mate, s)).wait_recv()
        in_wait(split - 1)
        in_wait(split)

        def relay(k, carry):
            up = k - up_late
            down = k - down_late

            @pl.when(both(up >= 0, within(split + up, lo_a, hi_a)))
            def _():
                in_wait(split + up + 1)
                a_row(split + up)

            @pl.when(both(down >= 0, within(split - 1 - down, lo_a, hi_a)))
            def _():
                in_wait(split - 2 - down)
                a_row(split - 1 - down)

            @pl.when(both(up >= up_from, within(split + up - 1, lo_b, hi_b)))
            def _():
                b_row(split + up - 1)

            @pl.when(both(down >= down_from, within(split - down, lo_b, hi_b)))
            def _():
                b_row(split - down)

            return carry

        lax.fori_loop(0, jnp.maximum(up_steps, down_steps), relay, 0)
        co[...] = cb[FINE : FINE + ROWS]

    @pl.when(even)
    def _():
        def wait_a(x, carry):
            a_copy(x).wait_recv()
            return carry

        lax.fori_loop(0, ROWS, wait_a, 0)

    out[...] = lax.dot_general(
        co[...].reshape(ROWS * NZ, NY),
        perm[...],
        (((1,), (1,)), ((), ())),
        precision=HIGH,
        preferred_element_type=jnp.float32,
    ).reshape(1, ROWS, NZ, NY)

    each_zone_copy(sent)
    each_piece(sent)
    each_state_copy(0, sent)
    each_state_copy(1, sent)
    for side in range(2):
        each_forward(side, lambda side, number: forward_copy(side, number).wait_send())
    for side, flag, is_far in sides:

        @pl.when(flag)
        def _():
            z_mate(side).wait_send()

            @pl.when(both(is_far, goes_on))
            def _():
                for part in range(BLOCK // PIECE):
                    z_next(side, part).wait_send()

    each_jump_copy(sent)
    each_jump_relay(sent)

    @pl.when(even)
    def _():
        j_mate().wait_send()

    @pl.when(odd)
    def _():
        def drain_a(x, carry):
            a_copy(x).wait_send()
            return carry

        lax.fori_loop(0, ROWS, drain_a, 0)

        @pl.when(passes_on)
        def _():
            def drain(x, carry):
                c_copy(x).wait_send()
                return carry

            lax.fori_loop(lo_b, hi_b + 1, drain, 0)


def shards(
    starts, zone_map, zone_velocity, conductivity, x_velocity, cross_velocity, coarse_kernel
):
    smem = pl.BlockSpec(memory_space=pltpu.SMEM)
    vmem = pl.BlockSpec(memory_space=pltpu.VMEM)
    field = lambda rows: pltpu.VMEM((rows, NZ, NY), jnp.float32)
    dma = pltpu.SemaphoreType.DMA
    return pl.pallas_call(
        kernel,
        name="parareal",
        out_shape=jax.ShapeDtypeStruct(starts.shape, jnp.float32),
        in_specs=[smem] * 5 + [vmem] * 2,
        out_specs=vmem,
        scratch_shapes=[
            pltpu.VMEM((NY, NY), jnp.float32),
            pltpu.VMEM((2, WIDE, NZ, NY), jnp.float32),
            field(ROWS),
            field(EXT),
            pltpu.VMEM((7, WIDE, NZ, NY), jnp.float32),
            field(ROWS),
            field(EXT),
            field(EXT),
            field(EXT),
            field(EXT),
            field(EXT),
            field(ROWS),
            field(4),
            dma((2, 2)),
            dma((2, 2)),
            dma((2, BLOCK // PIECE)),
            dma((2, BLOCK // PIECE)),
            dma((2,)),
            dma((2,)),
            dma((BLOCK // PIECE,)),
            dma((11,)),
            dma((2,)),
            dma((2,)),
            dma((2, ROWS)),
            dma((EXT,)),
            dma((2, ROWS)),
            dma((EXT,)),
            dma,
            dma,
            dma((EXT,)),
            dma((EXT,)),
            dma((ROWS,)),
            dma((ROWS,)),
        ],
        compiler_params=pltpu.CompilerParams(
            collective_id=0, has_side_effects=True, vmem_limit_bytes=56 * 2**20
        ),
    )(
        zone_velocity, conductivity, x_velocity, cross_velocity, coarse_kernel, starts, zone_map
    )


def solution(mesh):
    in_specs = (P("tm", "space", None, None), P("space", None, None), P(), P(), P(), P(), P())
    out_specs = P("tm", "space", None, None)
    return jax.shard_map(shards, mesh=mesh, in_specs=in_specs, out_specs=out_specs, check_vma=False)
```

```python
import functools

import jax
import jax.numpy as jnp
from jax import lax
from jax.experimental import pallas as pl
from jax.experimental.pallas import tpu as pltpu
from jax.sharding import PartitionSpec as P

FINE = 16
ZONES = 16
ROWS = 16
NZ = 16
NY = 512
TILES = 4
LANES = 128
EXT = ROWS + 2 * FINE
BLOCK = 8
PIECE = 2
PAD = 24
WIDE = ROWS + 2 * PAD
MESH = pl.DeviceIdType.MESH
HIGH = lax.Precision.HIGHEST


def iotas(shape):
    return lax.broadcasted_iota(jnp.int32, shape, 0), lax.broadcasted_iota(jnp.int32, shape, 1)


def shift_down(v):
    return jnp.concatenate([pltpu.roll(v[:, NY - LANES :], 1, 1), v[:, : NY - LANES]], axis=1)


def shift_up(v):
    return jnp.concatenate([v[:, LANES:], pltpu.roll(v[:, :LANES], LANES - 1, 1)], axis=1)


def coarse_row(src, x, ck):
    zi, li = iotas((NZ, LANES))
    sums = [[], [], []]
    for tile in range(TILES):
        part = [None] * 3
        for a in range(3):
            v = src[x + a - 1, :, tile * LANES : (tile + 1) * LANES]
            below = jnp.where(zi == 0, 0.0, pltpu.roll(v, 1, 0))
            above = jnp.where(zi == NZ - 1, 0.0, pltpu.roll(v, NZ - 1, 0))
            for b, w in enumerate((below, v, above)):
                for c in range(3):
                    term = ck[a, b, c] * w
                    part[c] = term if part[c] is None else part[c] + term
        for c in range(3):
            sums[c].append(part[c])
    low = [jnp.where(li == 0, 0.0, pltpu.roll(sums[0][TILES - 1], 1, 1))] + sums[0][:-1]
    high = sums[2][1:] + [jnp.where(li == LANES - 1, 0.0, pltpu.roll(sums[2][0], LANES - 1, 1))]
    return jnp.concatenate([low[j] + sums[1][j] + high[j] for j in range(TILES)], axis=1)


def kernel(
    zv, cond, xv, cv, ck, starts, zmap, out,
    perm, u, first, zone, w, gs, ja, jb, cin, ca, cb, co, rbuf,
    u_send, u_recv, z_send, z_recv, zm_send, zm_recv, zf_send, r_send, r_recv, f_send,
    ja_send, ja_recv, jb_send, jb_recv, jm_send, jm_recv, c_send, c_recv, a_send, a_recv,
):
    t = lax.axis_index("tm")
    s = lax.axis_index("space")
    slices = lax.axis_size("tm")
    parts = lax.axis_size("space")
    chips = slices // 2
    chip = t // 2
    core = lax.rem(t, 2)
    odd = core == 1
    even = core == 0
    has_low = s > 0
    has_high = s < parts - 1
    mate = t + 1 - 2 * core
    half = parts // 2
    far_low = s == half
    far_high = s == half - 1
    far = jnp.logical_or(far_low, far_high)
    over = jnp.where(far_low, s - 1, s + 1)
    ascending = s < half
    end_chip = jnp.logical_or(chip == 0, chip == chips - 1)
    seeds = jnp.logical_and(far, end_chip)
    across = 2 * (chips - 1 - chip) + core
    goes_on = jnp.logical_and(
        far, jnp.logical_and(chip != chips // 2 - 1, chip != chips // 2)
    )
    next_t = jnp.where(chip < chips // 2, t + 2, t - 2)
    last_t = jnp.where(chip < chips // 2, t - 2, t + 2)
    columns = (half - 4, half - 13, half - 12, half - 15)
    helpers = (columns, tuple(parts - 1 - h for h in columns))

    own_column = sum(
        jnp.where(chip == n, h, 0) for n, h in enumerate((half - 8, half - 5, half - 6, half - 7))
    )
    jump_helper = (own_column, parts - 1 - own_column)
    by_column = chip < 4

    def any_of(flags):
        return functools.reduce(jnp.logical_or, flags)

    helps_up = any_of([s == h for h in helpers[0]])
    helps_down = any_of([s == h for h in helpers[1]])

    def at(tm, space):
        return {"tm": tm, "space": space}

    def both(a, b):
        return jnp.logical_and(a, b)

    def remote(src, dst, send, recv, device):
        return pltpu.make_async_remote_copy(
            src_ref=src,
            dst_ref=dst,
            send_sem=send,
            recv_sem=recv,
            device_id=device,
            device_id_type=MESH,
        )

    barrier = pltpu.get_barrier_semaphore()

    def greet(tm, space):
        pl.semaphore_signal(barrier, inc=1, device_id=at(tm, space), device_id_type=MESH)

    @pl.when(far)
    def _():
        @pl.when(end_chip)
        def _():
            greet(across, over)

        @pl.when(jnp.logical_not(end_chip))
        def _():
            greet(last_t, s)

    @pl.when(jnp.logical_or(helps_up, helps_down))
    def _():
        greet(t, jnp.where(helps_up, half - 1, half))

    @pl.when(has_low)
    def _():
        greet(t, s - 1)

    @pl.when(has_high)
    def _():
        greet(t, s + 1)

    @pl.when(both(odd, has_low))
    def _():
        greet(t - 1, s - 1)

    @pl.when(both(odd, has_high))
    def _():
        greet(t - 1, s + 1)

    for side in range(2):

        @pl.when(both(both(even, by_column), s == jump_helper[side]))
        def _():
            greet(t + 1, half - 1 if side == 0 else half)

    greet(mate, s)

    @pl.when(both(odd, t >= 3))
    def _():
        greet(t - 2, s)

    yi, pi = iotas((NY, NY))
    perm[...] = jnp.where(yi == TILES * lax.rem(pi, LANES) + pi // LANES, 1.0, 0.0)
    own = starts[0].reshape(ROWS * NZ, NY)
    zone[FINE : FINE + ROWS] = jnp.dot(
        zmap[...].reshape(ROWS * NZ, NY).astype(jnp.float32),
        perm[...],
        preferred_element_type=jnp.float32,
    ).reshape(ROWS, NZ, NY)
    initial = jnp.dot(
        own, perm[...], precision=HIGH, preferred_element_type=jnp.float32
    ).reshape(ROWS, NZ, NY)
    u[0, PAD : PAD + ROWS] = initial
    first[...] = initial

    zero_row = jnp.zeros((NZ, NY), jnp.float32)

    def clear(begin, edge):
        cin[edge] = zero_row
        ca[edge] = zero_row

        def row(x, carry):
            u[0, x] = zero_row
            u[1, x] = zero_row
            for n in range(7):
                w[n, x] = zero_row
            return carry

        lax.fori_loop(begin, begin + PAD - 4, row, 0)

    @pl.when(jnp.logical_not(has_low))
    def _():
        clear(4, FINE - 1)

    @pl.when(jnp.logical_not(has_high))
    def _():
        clear(PAD + ROWS, FINE + ROWS)

    def count(flag):
        return flag.astype(jnp.int32)

    near = count(has_low) + count(has_high)
    pl.semaphore_wait(
        barrier,
        near
        + jnp.where(even, near, 0)
        + 1
        + count(both(odd, t < slices - 1))
        + count(seeds)
        + count(goes_on)
        + len(helpers[0]) * count(far)
        + count(both(far, both(odd, by_column))),
    )

    def z_half(side, c):
        at_row = FINE - BLOCK - BLOCK * c if side == 0 else FINE + ROWS + BLOCK * c
        return zone.at[pl.ds(at_row, BLOCK)]

    def z_copy(side, tm, space, part):
        source = FINE + BLOCK - BLOCK * core if side == 0 else FINE + BLOCK * core
        return remote(
            zone.at[pl.ds(source + PIECE * part, PIECE)],
            z_half(side, core).at[pl.ds(PIECE * part, PIECE)],
            z_send.at[side, part],
            z_recv.at[side, part],
            at(tm, space),
        )

    def z_mate(side):
        return remote(
            z_half(side, core), z_half(side, core), zm_send.at[side], zm_recv.at[side], at(mate, s)
        )

    def z_mate_wait(side):
        part = z_half(side, 1 - core)
        remote(part, part, zm_send.at[side], zm_recv.at[side], at(mate, s)).wait_recv()

    def z_next(side, part):
        rows = z_half(side, core).at[pl.ds(PIECE * part, PIECE)]
        return remote(rows, rows, zf_send.at[part], z_recv.at[side, part], at(next_t, s))

    def each_zone_copy(act):
        @pl.when(both(far_high, end_chip))
        def _():
            for part in range(BLOCK // PIECE):
                act(z_copy(0, across, s + 1, part))

        @pl.when(both(far_low, end_chip))
        def _():
            for part in range(BLOCK // PIECE):
                act(z_copy(1, across, s - 1, part))

        @pl.when(both(has_high, jnp.logical_not(far_high)))
        def _():
            for part in range(BLOCK // PIECE):
                act(z_copy(0, t, s + 1, part))

        @pl.when(both(has_low, jnp.logical_not(far_low)))
        def _():
            for part in range(BLOCK // PIECE):
                act(z_copy(1, t, s - 1, part))

    def u_rows(start_row, rows):
        return u.at[0, pl.ds(PAD + start_row, rows)]

    def u_copy(side, batch):
        if side == 0:
            source, to, space = BLOCK - BLOCK * batch, -BLOCK - BLOCK * batch, s + 1
        else:
            source, to, space = BLOCK * batch, ROWS + BLOCK * batch, s - 1
        return remote(
            first.at[pl.ds(source, BLOCK)],
            u_rows(to, BLOCK),
            u_send.at[side, batch],
            u_recv.at[side, batch],
            at(t, space),
        )

    pieces = (
        (0, 2, 2, 0),
        (0, 4, 1, 1),
        (0, 5, 2, 2),
        (0, 7, 1, 3),
        (0, 0, 2, -1),
        (1, 9, 2, 0),
        (1, 11, 2, 1),
        (1, 13, 1, 2),
        (1, 14, 2, 3),
        (1, 8, 1, -1),
    )

    def piece_copy(side, number):
        batch, skip, rows, helper = pieces[number]
        source = ROWS - skip - rows if side == 0 else skip
        to = -skip - rows if side == 0 else ROWS + skip
        if helper < 0:
            dst, recv, space = u_rows(to, rows), u_recv.at[side, batch], half if side == 0 else half - 1
        else:
            dst, recv = rbuf.at[pl.ds(2 * batch, rows)], r_recv.at[batch]
            space = helpers[side][helper]
        return remote(first.at[pl.ds(source, rows)], dst, r_send.at[number], recv, at(t, space))

    def forward_copy(side, number):
        batch, skip, rows, helper = pieces[number]
        to = -skip - rows if side == 0 else ROWS + skip
        return remote(
            rbuf.at[pl.ds(2 * batch, rows)],
            u_rows(to, rows),
            f_send.at[batch],
            u_recv.at[side, batch],
            at(t, half if side == 0 else half - 1),
        )

    def each_piece(act):
        for side, flag in ((0, far_high), (1, far_low)):

            @pl.when(flag)
            def _():
                for number in range(len(pieces)):
                    act(piece_copy(side, number))

    def each_forward(side, act):
        for helper, space in enumerate(helpers[side]):

            @pl.when(s == space)
            def _():
                for number in range(len(pieces)):
                    if pieces[number][3] == helper:
                        act(side, number)

    def each_state_copy(batch, act):
        @pl.when(both(has_high, jnp.logical_not(far_high)))
        def _():
            act(u_copy(0, batch))

        @pl.when(both(has_low, jnp.logical_not(far_low)))
        def _():
            act(u_copy(1, batch))

    start = lambda copy: copy.start()
    sent = lambda copy: copy.wait_send()
    each_piece(start)
    each_zone_copy(start)
    each_state_copy(0, start)
    each_state_copy(1, start)

    numbers = []
    for q in range(ZONES):
        v = zv[q]
        numbers.append((cond[q], xv[v], cv[1, v], cv[0, v]))
    zi, li = iotas((NZ, LANES))

    def weights(x, carry):
        for tile in range(TILES):
            sl = slice(tile * LANES, (tile + 1) * LANES)
            z = zone[FINE + x, :, sl].astype(jnp.int32)
            bits = [(z & (1 << b)) != 0 for b in range(4)]
            found = []
            for n in range(4):
                level = [numbers[q][n] for q in range(ZONES)]
                for b in range(4):
                    level = [
                        jnp.where(bits[b], level[2 * j + 1], level[2 * j])
                        for j in range(len(level) // 2)
                    ]
                found.append(level[0])
            d, cx, cz, cy = found
            xm = d + jnp.maximum(cx, 0.0)
            xp = d - jnp.minimum(cx, 0.0)
            zm = d + jnp.maximum(cz, 0.0)
            zp = d - jnp.minimum(cz, 0.0)
            ym = d + jnp.maximum(cy, 0.0)
            yp = d - jnp.minimum(cy, 0.0)
            w[0, PAD + x, :, sl] = 1.0 - (((xm + xp) + (zm + zp)) + (ym + yp))
            w[1, PAD + x, :, sl] = xm
            w[2, PAD + x, :, sl] = xp
            w[3, PAD + x, :, sl] = jnp.where(zi == 0, 0.0, zm)
            w[4, PAD + x, :, sl] = jnp.where(zi == NZ - 1, 0.0, zp)
            if tile == 0:
                ym = jnp.where(li == 0, 0.0, ym)
            if tile == TILES - 1:
                yp = jnp.where(li == LANES - 1, 0.0, yp)
            w[5, PAD + x, :, sl] = ym
            w[6, PAD + x, :, sl] = yp
        return carry

    lax.fori_loop(0, ROWS, weights, 0)

    def start_coarse(x):
        gs[x] = coarse_row(u.at[0], PAD + x, ck)

    def two_coarse(n, carry):
        start_coarse(2 * n + 1)
        start_coarse(2 * n + 2)
        return carry

    lax.fori_loop(0, ROWS // 2 - 1, two_coarse, 0)

    def forward(side, number):
        piece_copy(side, number).wait_recv()
        forward_copy(side, number).start()

    each_forward(1, forward)

    sides = ((0, has_low, far_low), (1, has_high, far_high))

    def take_zones(side, hand_on):
        for part in range(BLOCK // PIECE):
            z_copy(side, t, s, part).wait_recv()

            @pl.when(hand_on)
            def _():
                z_next(side, part).start()

        z_mate(side).start()

    def side_weights(side):
        z_mate_wait(side)
        lax.fori_loop(-FINE if side == 0 else ROWS, 0 if side == 0 else ROWS + FINE, weights, 0)

    for side, flag, is_far in sides:

        @pl.when(both(flag, jnp.logical_not(is_far)))
        def _():
            take_zones(side, False)

    for side, flag, is_far in sides:

        @pl.when(both(flag, jnp.logical_not(is_far)))
        def _():
            side_weights(side)

    for side, flag, is_far in sides:

        @pl.when(both(is_far, goes_on))
        def _():
            take_zones(side, True)

    each_forward(0, forward)

    def state_wait(side, batch):
        u_copy(side, batch).wait_recv()

    def early(batch):
        @pl.when(both(ascending, has_low))
        def _():
            state_wait(0, batch)

        @pl.when(both(jnp.logical_not(ascending), has_high))
        def _():
            state_wait(1, batch)

    early(0)

    @pl.when(ascending)
    def _():
        start_coarse(0)

    @pl.when(jnp.logical_not(ascending))
    def _():
        start_coarse(ROWS - 1)

    def block(src, dst, x0, count=BLOCK):
        base = PAD + jnp.where(ascending, x0, ROWS - count - x0)
        rows = [
            [src[base + r - 1, :, j * LANES : (j + 1) * LANES] for j in range(TILES)]
            for r in range(count + 2)
        ]
        for r in range(count):
            x = base + r
            v = rows[r + 1]
            low = [pltpu.roll(v[TILES - 1], 1, 1)] + v[:-1]
            high = v[1:] + [pltpu.roll(v[0], LANES - 1, 1)]
            for j in range(TILES):
                sl = slice(j * LANES, (j + 1) * LANES)
                centre = w[0, x, :, sl] * v[j]
                along_x = w[1, x, :, sl] * rows[r][j] + w[2, x, :, sl] * rows[r + 2][j]
                along_y = w[5, x, :, sl] * low[j] + w[6, x, :, sl] * high[j]
                along_z = w[3, x, :, sl] * pltpu.roll(v[j], 1, 0) + w[4, x, :, sl] * pltpu.roll(
                    v[j], NZ - 1, 0
                )
                dst[x, :, sl] = (centre + along_x) + (along_y + along_z)

    for level in range(1, ROWS - BLOCK // 2):
        src, dst = u.at[(level + 1) % 2], u.at[level % 2]

        def two_rows(m, carry):
            block(src, dst, level - BLOCK + 2 * m, 2)
            return carry

        pairs = BLOCK + 4 - level
        lax.fori_loop(0, pairs, two_rows, 0, unroll=3 if pairs % 3 == 0 else (2 if pairs % 2 == 0 else 1))

    early(1)

    def wedge(n, carry):
        for src, dst, level in ((u.at[0], u.at[1], 2 * n + 1), (u.at[1], u.at[0], 2 * n + 2)):
            block(src, dst, jnp.minimum(level - FINE, BLOCK - level))
        return carry

    lax.fori_loop(0, FINE // 2, wedge, 0)

    def slab(x0):
        def pair(n, carry):
            block(u.at[0], u.at[1], x0 - 2 * n - 1)
            block(u.at[1], u.at[0], x0 - 2 * n - 2)
            return carry

        lax.fori_loop(0, FINE // 2, pair, 0)

    for side, flag, is_far in sides:

        @pl.when(both(is_far, jnp.logical_not(goes_on)))
        def _():
            take_zones(side, False)

        @pl.when(is_far)
        def _():
            side_weights(side)

    @pl.when(ascending)
    def _():
        state_wait(1, 0)
        start_coarse(ROWS - 1)

    @pl.when(jnp.logical_not(ascending))
    def _():
        state_wait(0, 0)
        start_coarse(0)

    slab(ROWS)

    @pl.when(ascending)
    def _():
        state_wait(1, 1)

    @pl.when(jnp.logical_not(ascending))
    def _():
        state_wait(0, 1)

    slab(ROWS + BLOCK)

    keep = jnp.where(t == 0, 0.0, 1.0).astype(jnp.float32)
    depth = slices - 1 - 2 * chip

    def jump(x):
        return u[0, PAD + x] - keep * gs[x]

    def jump_loop(buf):
        def row(x, carry):
            buf[FINE + x] = jump(x)
            return carry

        lax.fori_loop(0, ROWS, row, 0)

    @pl.when(even)
    def _():
        jump_loop(ja)

    @pl.when(odd)
    def _():
        jump_loop(jb)

    def j_mate():
        part = ja.at[pl.ds(FINE, ROWS)]
        return remote(part, part, jm_send, jm_recv, at(mate, s))

    def j_copy(x, up, on_even):
        buf = ja if on_even else jb
        send, recv = (ja_send, ja_recv) if on_even else (jb_send, jb_recv)
        to = FINE + (x - ROWS if up else x + ROWS)
        if on_even:
            device = at(t + 1, s + 1 if up else s - 1)
        else:
            crosses = both(far_high if up else far_low, by_column)
            device = at(
                jnp.where(crosses, t - 1, t),
                jnp.where(crosses, jump_helper[0 if up else 1], s + 1 if up else s - 1),
            )
        return remote(buf.at[FINE + x], buf.at[to], send.at[1 if up else 0, x], recv.at[to], device)

    def jump_relay(n, up):
        x = ROWS - 1 - n if up else n
        to = FINE + (x - ROWS if up else x + ROWS)
        return remote(
            jb.at[to],
            jb.at[to],
            jb_send.at[1 if up else 0, x],
            jb_recv.at[to],
            at(t + 1, half if up else half - 1),
        )

    def each_jump_relay(act):
        for up in (True, False):

            @pl.when(both(both(even, by_column), s == jump_helper[0 if up else 1]))
            def _():
                def row(n, carry):
                    act(jump_relay(n, up))
                    return carry

                lax.fori_loop(0, depth - 1, row, 0)

    def each_jump_copy(act):
        for on_even, flag, rows in ((True, even, depth), (False, odd, depth - 1)):

            @pl.when(flag)
            def _():
                def row(n, carry):
                    @pl.when(has_high)
                    def _():
                        act(j_copy(ROWS - 1 - n, True, on_even))

                    @pl.when(has_low)
                    def _():
                        act(j_copy(n, False, on_even))

                    return carry

                lax.fori_loop(0, rows, row, 0)

    @pl.when(even)
    def _():
        j_mate().start()

    each_jump_copy(start)

    def relay_jump(copy):
        copy.wait_recv()
        copy.start()

    each_jump_relay(relay_jump)

    low_end = jnp.where(has_low, -FINE, 0)
    high_end = jnp.where(has_high, ROWS + FINE - 1, ROWS - 1)
    lo_a = jnp.maximum(-depth, low_end)
    hi_a = jnp.minimum(ROWS - 1 + depth, high_end)
    lo_b = jnp.maximum(1 - depth, low_end)
    hi_b = jnp.minimum(ROWS - 2 + depth, high_end)
    lo_i = jnp.maximum(-depth - 1, low_end)
    hi_i = jnp.minimum(ROWS + depth, high_end)
    passes_on = t < slices - 1
    split = jnp.where(far_high, ROWS - 2 * chip, jnp.where(far_low, 2 * chip, ROWS // 2))
    up_late = jnp.where(far_high, split - lo_a + 1, 0)
    down_late = jnp.where(far_low, hi_a - split + 2, 0)
    up_from = jnp.where(far_high, 0, jnp.where(far_low, 2, 1))
    down_from = jnp.where(far_low, 0, jnp.where(far_high, 2, 1))
    up_steps = up_late + jnp.maximum(hi_a - split, hi_b + 1 - split) + 1
    down_steps = down_late + jnp.maximum(split - 1 - lo_a, split - lo_b) + 1

    def c_copy(x):
        return remote(
            cb.at[FINE + x],
            cin.at[FINE + x],
            c_send.at[FINE + x],
            c_recv.at[FINE + x],
            at(t + 2, s),
        )

    def a_copy(x):
        return remote(ca.at[FINE + x], co.at[x], a_send.at[x], a_recv.at[x], at(mate, s))

    def j_wait(x, on_even):
        buf, recv = (ja, ja_recv) if on_even else (jb, jb_recv)
        remote(
            buf.at[FINE + x],
            buf.at[FINE + x],
            (ja_send if on_even else jb_send).at[0, 0],
            recv.at[FINE + x],
            at(t, s),
        ).wait_recv()

    def within(x, lo, hi):
        return both(x >= lo, x <= hi)

    def outside(x):
        return jnp.logical_or(x < 0, x >= ROWS)

    def in_wait(x):
        @pl.when(both(chip > 0, within(x, lo_i, hi_i)))
        def _():
            c_copy(x).wait_recv()

    def a_row(x):
        @pl.when(outside(x))
        def _():
            j_wait(x, True)

        @pl.when(chip == 0)
        def _():
            ca[FINE + x] = ja[FINE + x]

        @pl.when(chip > 0)
        def _():
            ca[FINE + x] = coarse_row(cin, FINE + x, ck) + ja[FINE + x]

        @pl.when(jnp.logical_not(outside(x)))
        def _():
            a_copy(x).start()

    def b_row(x):
        @pl.when(outside(x))
        def _():
            j_wait(x, False)

        cb[FINE + x] = coarse_row(ca, FINE + x, ck) + jb[FINE + x]

        @pl.when(passes_on)
        def _():
            c_copy(x).start()

    @pl.when(odd)
    def _():
        jm_wait = ja.at[pl.ds(FINE, ROWS)]
        remote(jm_wait, jm_wait, jm_send, jm_recv, at(mate, s)).wait_recv()
        in_wait(split - 1)
        in_wait(split)

        def relay(k, carry):
            up = k - up_late
            down = k - down_late

            @pl.when(both(up >= 0, within(split + up, lo_a, hi_a)))
            def _():
                in_wait(split + up + 1)
                a_row(split + up)

            @pl.when(both(down >= 0, within(split - 1 - down, lo_a, hi_a)))
            def _():
                in_wait(split - 2 - down)
                a_row(split - 1 - down)

            @pl.when(both(up >= up_from, within(split + up - 1, lo_b, hi_b)))
            def _():
                b_row(split + up - 1)

            @pl.when(both(down >= down_from, within(split - down, lo_b, hi_b)))
            def _():
                b_row(split - down)

            return carry

        lax.fori_loop(0, jnp.maximum(up_steps, down_steps), relay, 0)
        co[...] = cb[FINE : FINE + ROWS]

    @pl.when(even)
    def _():
        def wait_a(x, carry):
            a_copy(x).wait_recv()
            return carry

        lax.fori_loop(0, ROWS, wait_a, 0)

    out[...] = co[...]

    each_zone_copy(sent)
    each_piece(sent)
    each_state_copy(0, sent)
    each_state_copy(1, sent)
    for side in range(2):
        each_forward(side, lambda side, number: forward_copy(side, number).wait_send())
    for side, flag, is_far in sides:

        @pl.when(flag)
        def _():
            z_mate(side).wait_send()

            @pl.when(both(is_far, goes_on))
            def _():
                for part in range(BLOCK // PIECE):
                    z_next(side, part).wait_send()

    each_jump_copy(sent)
    each_jump_relay(sent)

    @pl.when(even)
    def _():
        j_mate().wait_send()

    @pl.when(odd)
    def _():
        def drain_a(x, carry):
            a_copy(x).wait_send()
            return carry

        lax.fori_loop(0, ROWS, drain_a, 0)

        @pl.when(passes_on)
        def _():
            def drain(x, carry):
                c_copy(x).wait_send()
                return carry

            lax.fori_loop(lo_b, hi_b + 1, drain, 0)


def in_order(ends, out):
    pi, yi = iotas((NY, NY))
    turn = jnp.where(yi == TILES * lax.rem(pi, LANES) + pi // LANES, 1.0, 0.0).astype(jnp.bfloat16)
    rest = ends[...].reshape(ROWS * NZ, NY)
    parts = []
    for _ in range(3):
        parts.append(rest.astype(jnp.bfloat16))
        rest = rest - parts[-1].astype(jnp.float32)
    low, mid, top = (
        jnp.dot(part, turn, preferred_element_type=jnp.float32) for part in reversed(parts)
    )
    out[...] = ((low + mid) + top).reshape(1, ROWS, NZ, NY)


def shards(
    starts, zone_map, zone_velocity, conductivity, x_velocity, cross_velocity, coarse_kernel
):
    smem = pl.BlockSpec(memory_space=pltpu.SMEM)
    vmem = pl.BlockSpec(memory_space=pltpu.VMEM)
    field = lambda rows: pltpu.VMEM((rows, NZ, NY), jnp.float32)
    dma = pltpu.SemaphoreType.DMA
    ends = pl.pallas_call(
        kernel,
        name="parareal",
        out_shape=jax.ShapeDtypeStruct(starts.shape[1:], jnp.float32),
        in_specs=[smem] * 5 + [vmem] * 2,
        out_specs=vmem,
        scratch_shapes=[
            pltpu.VMEM((NY, NY), jnp.float32),
            pltpu.VMEM((2, WIDE, NZ, NY), jnp.float32),
            field(ROWS),
            field(EXT),
            pltpu.VMEM((7, WIDE, NZ, NY), jnp.float32),
            field(ROWS),
            field(EXT),
            field(EXT),
            field(EXT),
            field(EXT),
            field(EXT),
            field(ROWS),
            field(4),
            dma((2, 2)),
            dma((2, 2)),
            dma((2, BLOCK // PIECE)),
            dma((2, BLOCK // PIECE)),
            dma((2,)),
            dma((2,)),
            dma((BLOCK // PIECE,)),
            dma((10,)),
            dma((2,)),
            dma((2,)),
            dma((2, ROWS)),
            dma((EXT,)),
            dma((2, ROWS)),
            dma((EXT,)),
            dma,
            dma,
            dma((EXT,)),
            dma((EXT,)),
            dma((ROWS,)),
            dma((ROWS,)),
        ],
        compiler_params=pltpu.CompilerParams(
            collective_id=0, has_side_effects=True, vmem_limit_bytes=56 * 2**20
        ),
    )(
        zone_velocity, conductivity, x_velocity, cross_velocity, coarse_kernel, starts, zone_map
    )
    return pl.pallas_call(
        in_order,
        name="in_order",
        out_shape=jax.ShapeDtypeStruct(starts.shape, jnp.float32),
        in_specs=[vmem],
        out_specs=vmem,
        compiler_params=pltpu.CompilerParams(vmem_limit_bytes=16 * 2**20),
    )(ends)


def solution(mesh):
    in_specs = (P("tm", "space", None, None), P("space", None, None), P(), P(), P(), P(), P())
    out_specs = P("tm", "space", None, None)
    return jax.shard_map(shards, mesh=mesh, in_specs=in_specs, out_specs=out_specs, check_vma=False)
```
